32 devices in a mesh: rows: 4 (over y, x), cols: 8 (over z, core).
Axes of the slice: x: 2, y: 2, z: 4, core: 2. Of those that a mesh axis runs over, the one named last changes fastest.
Arguments:
- design: float32 [6, 8, 64], P(None, 'rows', 'cols'), may hold values from -6 to 6
- active: int32 [8, 64], P('rows', 'cols'), may hold values 0 or 1
- stamp_basis: float32 [6, 32, 32], replicated, may hold values from -2 to 2
- film_field: bfloat16 [16, 128, 1024], P(None, 'rows', 'cols'), may hold values from -6 to 6
- lift_weight: float32 [16], replicated, may hold values from -4 to 4
- lift_bias: float32 [16], replicated, may hold values from -3 to 3
- conv_weight: bfloat16 [4, 9, 16, 16], replicated, may hold values from -0.5 to 0.5
- conv_bias: float32 [4, 16], replicated, may hold values from -3 to 3
- readout: float32 [16], replicated, may hold values from -1.5 to 1.5
- target: float32 [128, 1024], P('rows', 'cols'), may hold values from -6 to 6
- dilation: int32 [4], replicated, may hold values from 1 to 8, as said below
Outputs:
- new_design: float32 [6, 8, 64], P(None, 'rows', 'cols')
- objective: float32 [2], replicated
The draws below stay inside these ranges and needn't reach their ends.
Inputs may be any that keep to these rules, and one draw needn't show every extreme that they name: The dilation of each layer is an integer from 1 to 8; some layer has exactly 8.
All inputs are finite; a program needn't handle non-finite values. No bound on the sum of `active` on one device may be relied on, other than what follows from the above.
Results may differ from the reference program's by a relative error of at most 0.0025.
Values may be sent and summed in bfloat16 or wider, within the bound.
A program may use at most 64 MiB of HBM per device.

```python
import jax
import jax.numpy as jnp
from jax import lax

CHANNELS = 16
NPARAM = 6
STRIDE = 16
DMAX = 8
LAYERS = 4
ITERS = 2
GR = 8
GC = 64
NR = 128
NC = 1024


def draw_dilation(key, part):
    levels = jax.random.randint(key, (LAYERS,), 1, DMAX + 1)
    chosen = jax.random.randint(jax.random.fold_in(key, 11), (), 0, LAYERS)
    return jnp.where(jnp.arange(LAYERS) == chosen, DMAX, levels).astype(jnp.int32)


def set_ends(array, own_key, low, largest):
    longest = array.shape.index(max(array.shape))
    spots = []
    for shift in (0, 1):
        where = [jax.random.randint(jax.random.fold_in(own_key, axis), (), 0, length) for axis, length in enumerate(array.shape)]
        where[longest] = (where[longest] + shift) % array.shape[longest]
        spots.append(tuple(where))
    return array.at[spots[0]].set(low).at[spots[1]].set(largest)


def shard_levels(key, shape, split, least, largest):
    level = 1.0
    for dim, parts in split:
        heights = jax.random.uniform(jax.random.fold_in(jax.random.fold_in(key, 6), dim), (parts,), jnp.float32, least / len(split), largest / len(split))
        level = level * jnp.repeat(jnp.exp(heights), shape[dim] // parts).reshape((-1,) + (1,) * (len(shape) - 1 - dim))
    return level


def normal_values(own_key, shape, deviation, limit, cuts=(), kind=jnp.bfloat16):
    values = deviation * jax.random.normal(own_key, shape, jnp.float32)
    if cuts:
        values = values * shard_levels(own_key, shape, cuts, -0.22, 0.18)
    return jnp.clip(values, -limit, limit).astype(kind)


def setup_inputs(seed: int = 0) -> dict:
    key_list = jax.random.split(jax.random.key(seed), 12)
    return {
        "design": normal_values(key_list[0], (NPARAM, GR, GC), 1.0, 6.0, ((1, 4), (2, 8)), jnp.float32),
        "active": set_ends((jax.random.randint(key_list[1], (GR, GC), 0, 4) < 3).astype(jnp.int32), jax.random.fold_in(key_list[1], 1), 0, 1),
        "stamp_basis": normal_values(key_list[2], (NPARAM, 2 * STRIDE, 2 * STRIDE), 0.25, 2.0, (), jnp.float32),
        "film_field": normal_values(key_list[3], (CHANNELS, NR, NC), 1.0, 6.0, ((1, 4), (2, 8))),
        "lift_weight": normal_values(key_list[4], (CHANNELS,), 1.0, 4.0, (), jnp.float32),
        "lift_bias": normal_values(key_list[5], (CHANNELS,), 0.5, 3.0, (), jnp.float32),
        "conv_weight": normal_values(key_list[6], (LAYERS, 9, CHANNELS, CHANNELS), (9 * CHANNELS) ** -0.5, 0.5),
        "conv_bias": normal_values(key_list[7], (LAYERS, CHANNELS), 0.5, 3.0, (), jnp.float32),
        "readout": normal_values(key_list[8], (CHANNELS,), CHANNELS ** -0.5, 1.5, (), jnp.float32),
        "target": normal_values(key_list[9], (NR, NC), 1.0, 6.0, ((0, 4), (1, 8)), jnp.float32),
        "dilation": draw_dilation(jax.random.fold_in(key_list[11], 71), 0),
    }


step_rate = 0.25
norm_eps = 1e-06

def tap_list():
    return [(row_step, col_step) for row_step in (-1, 0, 1) for col_step in (-1, 0, 1)]

def basis_blocks(stamp_basis):
    side = stamp_basis.shape[1] // 2
    padded_basis = jnp.pad(stamp_basis, ((0, 0), (side, side), (side, side)))
    pieces = []
    for row_step, col_step in tap_list():
        top = side + side // 2 - side * row_step
        left = side + side // 2 - side * col_step
        pieces.append(padded_basis[:, top:top + side, left:left + side])
    return jnp.stack(pieces)

def render(padded_amp, blocks, dimple_rows, dimple_cols):
    side = blocks.shape[2]
    shifted = jnp.stack([padded_amp[:, 1 + r:1 + r + dimple_rows, 1 + c:1 + c + dimple_cols] for r, c in tap_list()])
    tiles = jnp.einsum('tpab,tpyx->aybx', shifted, blocks, precision=lax.Precision.HIGHEST)
    return tiles.reshape(dimple_rows * side, dimple_cols * side)

def render_back(padded_grad, blocks, dimple_rows, dimple_cols):
    side = blocks.shape[2]
    framed = padded_grad.reshape(dimple_rows + 2, side, dimple_cols + 2, side)
    summed = jnp.zeros((blocks.shape[1], dimple_rows, dimple_cols), jnp.float32)
    for index, (r, c) in enumerate(tap_list()):
        window = framed[1 - r:1 - r + dimple_rows, :, 1 - c:1 - c + dimple_cols, :]
        summed = summed + jnp.einsum('aybx,pyx->pab', window, blocks[index], precision=lax.Precision.HIGHEST)
    return summed

def conv_forward(padded, weight, bias, dilate, out_rows, out_cols):
    channels = weight.shape[1]
    summed = jnp.zeros((channels, out_rows, out_cols), jnp.float32)
    zero = jnp.asarray(0, jnp.int32)
    for index, (r, c) in enumerate(tap_list()):
        window = lax.dynamic_slice(padded, (zero, (DMAX + r * dilate).astype(jnp.int32), (DMAX + c * dilate).astype(jnp.int32)), (channels, out_rows, out_cols))
        summed = summed + jnp.einsum('oc,chw->ohw', weight[index].astype(jnp.float32), window.astype(jnp.float32), precision=lax.Precision.HIGHEST)
    return summed + bias[:, None, None]

def conv_back(padded, weight, dilate, out_rows, out_cols):
    channels = weight.shape[1]
    summed = jnp.zeros((channels, out_rows, out_cols), jnp.float32)
    zero = jnp.asarray(0, jnp.int32)
    for index, (r, c) in enumerate(tap_list()):
        window = lax.dynamic_slice(padded, (zero, (DMAX - r * dilate).astype(jnp.int32), (DMAX - c * dilate).astype(jnp.int32)), (channels, out_rows, out_cols))
        summed = summed + jnp.einsum('oc,ohw->chw', weight[index].astype(jnp.float32), window.astype(jnp.float32), precision=lax.Precision.HIGHEST)
    return summed

def silu_slope(value):
    logistic = jax.nn.sigmoid(value)
    return logistic * (1.0 + value * (1.0 - logistic))

def reference(design, active, stamp_basis, film_field, lift_weight, lift_bias, conv_weight, conv_bias, readout, target, dilation):
    blocks = basis_blocks(stamp_basis)
    active_mask = active.astype(jnp.float32)
    cell_rows, cell_cols = target.shape
    params = design
    objectives = []
    for iteration in range(ITERS):
        amplitude = params * active_mask
        padded_amp = jnp.pad(amplitude, ((0, 0), (1, 1), (1, 1)))
        height = render(padded_amp, blocks, GR, GC)
        state = (lift_weight[:, None, None] * height[None] + lift_bias[:, None, None] + film_field.astype(jnp.float32)).astype(jnp.bfloat16)
        pres = []
        for layer in range(LAYERS):
            padded = jnp.pad(state, ((0, 0), (DMAX, DMAX), (DMAX, DMAX)))
            pre = conv_forward(padded, conv_weight[layer], conv_bias[layer], dilation[layer], cell_rows, cell_cols)
            pres.append(pre)
            state = (state.astype(jnp.float32) + jax.nn.silu(pre)).astype(jnp.bfloat16)
        pressure = lax.optimization_barrier(jnp.sum(readout[:, None, None] * state.astype(jnp.float32), axis=0))
        misfit = pressure - target
        objectives.append(0.5 * jnp.mean(misfit * misfit))
        adjoint = readout[:, None, None] * (misfit / (STRIDE * STRIDE))[None]
        for layer in range(LAYERS - 1, -1, -1):
            slope = (adjoint * silu_slope(pres[layer])).astype(jnp.bfloat16)
            padded = jnp.pad(slope, ((0, 0), (DMAX, DMAX), (DMAX, DMAX)))
            adjoint = adjoint + conv_back(padded, conv_weight[layer], dilation[layer], cell_rows, cell_cols)
        height_grad = lax.optimization_barrier(jnp.sum(lift_weight[:, None, None] * adjoint, axis=0))
        gradient = render_back(jnp.pad(height_grad, STRIDE), blocks, GR, GC) * active_mask
        mean_square = jnp.sum(gradient * gradient) / (NPARAM * GR * GC)
        params = params - step_rate * gradient / jnp.sqrt(mean_square + norm_eps)
    return (params, jnp.stack(objectives))
```

```python
import functools

import jax
import jax.numpy as jnp
import numpy as np
from jax import lax
from jax.experimental import pallas as pl
from jax.experimental.pallas import tpu as pltpu
from jax.sharding import PartitionSpec as P

DMAX = 8
LAYERS = 4
ITERS = 2
LANES = 128

step_rate = 0.25
norm_eps = 1e-06

MESH = pl.DeviceIdType.MESH
F32 = jnp.float32
BF16 = jnp.bfloat16
OTHERS = [0, 1, 2, 3, 5, 6, 7, 8]
PER_ITER = 2 * LAYERS + 2


def tap_list():
    return [(row_step, col_step) for row_step in (-1, 0, 1) for col_step in (-1, 0, 1)]


def split3(value):
    high = value.astype(BF16)
    rest = value - high.astype(F32)
    mid = rest.astype(BF16)
    low = (rest - mid.astype(F32)).astype(BF16)
    return high, mid, low


def exact_dot(a, b):
    return jnp.dot(a, b, precision=lax.Precision.HIGHEST, preferred_element_type=F32)


def exact_dot_nt(a, b):
    return lax.dot_general(
        a, b, (((1,), (1,)), ((), ())), precision=lax.Precision.HIGHEST, preferred_element_type=F32
    )


def kernel(
    cfg,
    dil_ref, design_ref, active_ref, film_ref, target_ref, lanes_ref, wt_ref, blk_ref, sel_ref, selt_ref,
    new_ref, obj_ref,
    center, halo_l, halo_r, edge_l, edge_r, state_s, x_s, wbig, pre_s, adj_s, ee_s,
    amp9, part, got, grad9, q_s, grad_t, ar, ar_src,
    send_sem, recv_sem, ar_send, ar_recv,
):
    nrow, ncol, rows, total_cells, total_entries = cfg
    ndev = nrow * ncol
    nx = rows * 16
    my_r = lax.axis_index("rows")
    my_c = lax.axis_index("cols")
    me = my_r * ncol + my_c

    def exists(m):
        dr, dc = m // 3 - 1, m % 3 - 1
        r, c = my_r + dr, my_c + dc
        return (r >= 0) & (r < nrow) & (c >= 0) & (c < ncol)

    def ident(m):
        dr, dc = m // 3 - 1, m % 3 - 1
        return (my_r + dr, my_c + dc)

    def desc(phase, m, src, dst):
        return pltpu.make_async_remote_copy(
            src_ref=src(m), dst_ref=dst(m),
            send_sem=send_sem.at[phase, m], recv_sem=recv_sem.at[phase, m],
            device_id=ident(m), device_id_type=MESH,
        )

    def start(phase, src, dst):
        for m in OTHERS:
            @pl.when(exists(m))
            def _():
                desc(phase, m, src, dst).start()

    def arrive(phase, src, dst):
        for m in OTHERS:
            @pl.when(exists(8 - m))
            def _():
                desc(phase, m, src, dst).wait_recv()

    def sent(phase, src, dst):
        for m in OTHERS:
            @pl.when(exists(m))
            def _():
                desc(phase, m, src, dst).wait_send()

    def state_refs(slot):
        c = center.at[slot]
        el, er, hl, hr = edge_l.at[slot], edge_r.at[slot], halo_l.at[slot], halo_r.at[slot]
        D, R = DMAX, rows

        def src(m):
            return {
                0: lambda: el.at[pl.ds(0, D)], 1: lambda: c.at[pl.ds(D, D)], 2: lambda: er.at[pl.ds(0, D)],
                3: lambda: el, 5: lambda: er,
                6: lambda: el.at[pl.ds(R - D, D)], 7: lambda: c.at[pl.ds(R, D)], 8: lambda: er.at[pl.ds(R - D, D)],
            }[m]()

        def dst(m):
            return {
                0: lambda: hr.at[pl.ds(R + D, D)], 1: lambda: c.at[pl.ds(R + D, D)], 2: lambda: hl.at[pl.ds(R + D, D)],
                3: lambda: hr.at[pl.ds(D, R)], 5: lambda: hl.at[pl.ds(D, R)],
                6: lambda: hr.at[pl.ds(0, D)], 7: lambda: c.at[pl.ds(0, D)], 8: lambda: hl.at[pl.ds(0, D)],
            }[m]()

        return src, dst

    def amp_refs(_):
        return (lambda m: amp9.at[4]), (lambda m: amp9.at[8 - m])

    def part_refs(it):
        return (lambda m: part.at[it, m]), (lambda m: got.at[it, 8 - m])

    def grad_refs(it):
        return (lambda m: grad_t.at[it]), (lambda m: grad9.at[it, 8 - m])

    nslot = ITERS * 2 * LAYERS

    def clear(slot, _):
        z = jnp.zeros((DMAX, 16, LANES), BF16)
        center[slot, 0:DMAX] = z
        center[slot, rows + DMAX : rows + 2 * DMAX] = z
        zh = jnp.zeros((rows + 2 * DMAX, LANES), F32)
        halo_l[slot] = zh
        halo_r[slot] = zh
        return 0

    lax.fori_loop(0, nslot, clear, 0)
    z9 = jnp.zeros((9, 16, LANES), F32)
    amp9[...] = z9
    for it in range(ITERS):
        got[it] = z9
        grad9[it] = z9
    amp9[4] = design_ref[...] * active_ref[...]

    barrier = pltpu.get_barrier_semaphore()

    def greet(k, _):
        other = lax.rem(me + k, ndev)
        pl.semaphore_signal(barrier, inc=1, device_id=(other // ncol, lax.rem(other, ncol)), device_id_type=MESH)
        return 0

    lax.fori_loop(1, ndev, greet, 0)
    pl.semaphore_wait(barrier, ndev - 1)

    amp_phase = ITERS * PER_ITER
    start(amp_phase, *amp_refs(0))

    lane = lax.broadcasted_iota(jnp.int32, (24, 16, LANES), 2) // 16
    jpos = lax.broadcasted_iota(jnp.int32, (24, 16, LANES), 0) - 8 - lane
    for l in range(LAYERS):
        d = dil_ref[l]
        masks = [jpos == rx * d for rx in (-1, 0, 1)]
        for f in range(2):
            for ry in range(3):
                acc = jnp.zeros((24, 16, LANES), F32)
                for rx in range(3):
                    w = wt_ref[f, l, 3 * ry + rx].astype(F32)
                    acc = jnp.where(masks[rx], w[None], acc)
                wbig[f, l, ry] = acc.astype(BF16).reshape(384, LANES)
    ones_block = (
        lax.broadcasted_iota(jnp.int32, (LANES, LANES), 0) // 16
        == lax.broadcasted_iota(jnp.int32, (LANES, LANES), 1) // 16
    ).astype(F32).astype(BF16)
    pos = lax.broadcasted_iota(jnp.int32, (LANES, 16 * LANES), 0)
    col = lax.broadcasted_iota(jnp.int32, (LANES, 16 * LANES), 1)
    ee_s[...] = (pos == (col // LANES) * 8 + (col % LANES) // 16).astype(F32).astype(BF16)

    lw = lanes_ref[0:1, :]
    lb = lanes_ref[1:2, :]
    ro = lanes_ref[2:3, :]
    bsub = lax.broadcasted_iota(jnp.int32, (rows + 2 * DMAX, 8, LANES), 1)

    def publish(slot, phase, value):
        state_s[...] = value.reshape(rows, 16, LANES)
        center[slot, DMAX : rows + DMAX] = value.astype(BF16).reshape(rows, 16, LANES)
        edge_l[slot] = state_s[:, 0, :]
        edge_r[slot] = state_s[:, 15, :]
        start(phase, *state_refs(slot))

    def conv(slot, phase, f, l):
        arrive(phase, *state_refs(slot))
        cb = center[slot]
        c = cb.astype(F32)
        c0, c1 = c[:, 0:8], c[:, 8:16]
        hl = halo_l[slot][:, None, :]
        hr = halo_r[slot][:, None, :]
        l0 = jnp.where(bsub == 0, hl, pltpu.roll(c1, 1, 1))
        r1 = jnp.where(bsub == 7, hr, pltpu.roll(c0, 7, 1))
        x_s[:, :, 0:128] = jnp.concatenate([l0, c0], axis=1).astype(BF16)
        x_s[:, :, 128:256] = cb
        x_s[:, :, 256:384] = jnp.concatenate([c1, r1], axis=1).astype(BF16)
        d = dil_ref[l]
        out = None
        for ry in range(3):
            lhs = x_s[pl.ds(DMAX + (ry - 1) * d, rows)].reshape(nx, 384)
            term = jnp.dot(lhs, wbig[f, l, ry], preferred_element_type=F32)
            out = term if out is None else out + term
        return out

    def sigmoid(v):
        return 1.0 / (1.0 + jnp.exp(-v))

    arrive(amp_phase, *amp_refs(0))
    sent(amp_phase, *amp_refs(0))

    def step(it, _):
        base = it * PER_ITER
        slot0 = it * 2 * LAYERS
        picked = exact_dot(sel_ref[...], amp9[...].reshape(144, LANES))
        height = jnp.zeros((16, 256), F32)
        for t in range(9):
            height = height + exact_dot(picked[16 * t : 16 * t + 16, 0:8], blk_ref[t])
        two = jnp.concatenate([height[:, 0:128], height[:, 128:256]], axis=0)
        spread = None
        for piece in split3(two):
            term = jnp.dot(piece, ee_s[...], preferred_element_type=F32)
            spread = term if spread is None else spread + term
        for s in range(2):
            for k in range(16):
                q = 16 * s + k
                y, xh = q // 2, q % 2
                for a in range(rows // 16):
                    v = spread[16 * s + 8 * a : 16 * s + 8 * a + 8, 128 * k : 128 * k + 128]
                    state_s[16 * a + y, 8 * xh : 8 * xh + 8, :] = v
        h = state_s[...].reshape(nx, LANES)
        state = (lw * h + lb + film_ref[...].astype(F32).reshape(nx, LANES)).astype(BF16).astype(F32)
        for l in range(LAYERS):
            publish(slot0 + l, base + l, state)
            pre = conv(slot0 + l, base + l, 0, l) + lanes_ref[4 + l : 5 + l, :]
            pre_s[l] = pre
            state = (state + pre * sigmoid(pre)).astype(BF16).astype(F32)
        pressure = None
        for piece in split3(ro * state):
            term = jnp.dot(piece, ones_block, preferred_element_type=F32)
            pressure = term if pressure is None else pressure + term
        misfit = pressure - target_ref[...].reshape(nx, LANES)
        miss = jnp.sum(misfit * misfit, keepdims=True) * (0.5 / 16)
        adjoint = ro * (misfit * (1.0 / 256.0))
        for n in range(LAYERS):
            l = LAYERS - 1 - n
            v = pre_s[l]
            s = sigmoid(v)
            slope = (adjoint * (s * (1.0 + v * (1.0 - s)))).astype(BF16).astype(F32)
            publish(slot0 + LAYERS + n, base + LAYERS + n, slope)
            adjoint = adjoint + conv(slot0 + LAYERS + n, base + LAYERS + n, 1, l)
        adj_s[...] = (lw * adjoint).reshape(rows, 16, LANES)
        strips = []
        for s in range(2):
            tiles = []
            for k in range(16):
                q = 16 * s + k
                y, xh = q // 2, q % 2
                tiles.append(
                    jnp.concatenate(
                        [adj_s[16 * a + y, 8 * xh : 8 * xh + 8, :] for a in range(rows // 16)], axis=0
                    )
                )
            strips.append(jnp.concatenate(tiles, axis=1))
        both = jnp.concatenate(strips, axis=0)
        folded = None
        for piece in split3(both):
            term = lax.dot_general(
                piece, ee_s[...], (((1,), (1,)), ((), ())), preferred_element_type=F32
            )
            folded = term if folded is None else folded + term
        hg = jnp.concatenate([folded[0:16], folded[16:32]], axis=1)
        q_s[...] = jnp.zeros((144, LANES), F32)
        for t in range(9):
            q_s[16 * t : 16 * t + 16, 0:8] = exact_dot_nt(hg, blk_ref[t])
        mine = exact_dot(selt_ref[...], q_s[...]).reshape(9, 16, LANES)
        part[it] = mine
        p_phase = base + 2 * LAYERS
        start(p_phase, *part_refs(it))
        got[it, 4] = mine[4]
        arrive(p_phase, *part_refs(it))
        gradient = jnp.sum(got[it], axis=0) * active_ref[...]
        grad_t[it] = gradient
        squares = jnp.sum(gradient * gradient, keepdims=True)
        sub = lax.broadcasted_iota(jnp.int32, (8, LANES), 0)
        tile = jnp.where(sub == 0, squares, miss)
        ar_src[it] = tile
        g_phase = p_phase + 1

        def tell(k, _):
            other = lax.rem(me + k, ndev)
            pltpu.make_async_remote_copy(
                src_ref=ar_src.at[it], dst_ref=ar.at[it, me],
                send_sem=ar_send.at[it], recv_sem=ar_recv.at[it],
                device_id=(other // ncol, lax.rem(other, ncol)), device_id_type=MESH,
            ).start()
            return 0

        lax.fori_loop(1, ndev, tell, 0)
        start(g_phase, *grad_refs(it))
        ar[it, me] = tile
        many = ar.at[it, pl.ds(0, ndev - 1)]
        pltpu.make_async_copy(many, many, ar_recv.at[it]).wait()
        arrive(g_phase, *grad_refs(it))
        total = jnp.sum(ar[it], axis=0)
        scale = step_rate / jnp.sqrt(total[0:1] * (1.0 / total_entries) + norm_eps)
        obj_ref[it] = total * (1.0 / total_cells)
        grad9[it, 4] = gradient
        amp9[...] = amp9[...] - grad9[it] * scale[None]
        new_ref[...] = new_ref[...] - gradient * scale
        return 0

    new_ref[...] = design_ref[...]
    lax.fori_loop(0, ITERS, step, 0)

    def drain(it, _):
        base = it * PER_ITER
        for n in range(2 * LAYERS):
            sent(base + n, *state_refs(it * 2 * LAYERS + n))
        sent(base + 2 * LAYERS, *part_refs(it))
        sent(base + 2 * LAYERS + 1, *grad_refs(it))
        many = ar.at[it, pl.ds(0, ndev - 1)]
        pltpu.make_async_copy(many, many, ar_send.at[it]).wait()
        return 0

    lax.fori_loop(0, ITERS, drain, 0)


def select_matrix(dr_count, dc_count):
    sel = np.zeros((9, dr_count, dc_count, 9, dr_count, dc_count), np.float32)
    for t, (ry, rx) in enumerate(tap_list()):
        for a in range(dr_count):
            for b in range(dc_count):
                ta, tb = a + ry, b + rx
                nr, nc = ta // dr_count, tb // dc_count
                sel[t, a, b, 3 * (nr + 1) + nc + 1, ta - nr * dr_count, tb - nc * dc_count] = 1
    size = 9 * dr_count * dc_count
    return sel.reshape(size, size)


def basis_blocks(stamp_basis):
    side = stamp_basis.shape[1] // 2
    padded_basis = jnp.pad(stamp_basis, ((0, 0), (side, side), (side, side)))
    pieces = []
    for row_step, col_step in tap_list():
        top = side + side // 2 - side * row_step
        left = side + side // 2 - side * col_step
        pieces.append(padded_basis[:, top : top + side, left : left + side])
    return jnp.stack(pieces)


def on_device(
    design, active, stamp_basis, film_field, lift_weight, lift_bias, conv_weight, conv_bias, readout, target, dilation
):
    channels, rows, cols = film_field.shape
    nparams, drows, dcols = design.shape
    nrow = lax.axis_size("rows")
    ncol = lax.axis_size("cols")
    ndev = nrow * ncol
    total_cells = rows * cols * ndev
    total_entries = nparams * drows * dcols * ndev

    def by_dimple(v):
        v = v.reshape(nparams, drows * dcols).T
        return jnp.pad(v, ((0, 0), (0, LANES - nparams)))

    design_t = by_dimple(design)
    active_t = jnp.broadcast_to(active.astype(F32).reshape(drows * dcols, 1), (drows * dcols, LANES))
    film = film_field.reshape(channels, rows, dcols, 2, 8).transpose(1, 3, 2, 4, 0).reshape(rows, 16, LANES)
    targ = target.reshape(rows, dcols, 2, 8).transpose(0, 2, 1, 3).reshape(rows, 16, 8, 1)
    targ = jnp.broadcast_to(targ, (rows, 16, 8, 16)).reshape(rows, 16, LANES)
    lanes = jnp.concatenate(
        [jnp.tile(jnp.stack([lift_weight, lift_bias, readout, readout]), (1, 8)), jnp.tile(conv_bias, (1, 8))]
    )
    wt = jnp.stack([jnp.swapaxes(conv_weight, 2, 3), conv_weight[:, ::-1]])
    wt = jnp.tile(wt, (1, 1, 1, 1, 8))
    blocks = jnp.pad(basis_blocks(stamp_basis), ((0, 0), (0, 8 - nparams), (0, 0), (0, 0))).reshape(9, 8, 256)
    sel = select_matrix(drows, dcols)

    nslot = ITERS * 2 * LAYERS
    phases = ITERS * PER_ITER + 1
    tall = rows + 2 * DMAX
    vmem = pl.BlockSpec(memory_space=pltpu.VMEM)
    new, obj = pl.pallas_call(
        functools.partial(kernel, (nrow, ncol, rows, total_cells, total_entries)),
        out_shape=(
            jax.ShapeDtypeStruct((16, LANES), F32),
            jax.ShapeDtypeStruct((ITERS, 8, LANES), F32),
        ),
        in_specs=[pl.BlockSpec(memory_space=pltpu.SMEM)] + [vmem] * 9,
        out_specs=(vmem, vmem),
        scratch_shapes=[
            pltpu.VMEM((nslot, tall, 16, LANES), BF16),
            pltpu.VMEM((nslot, tall, LANES), F32),
            pltpu.VMEM((nslot, tall, LANES), F32),
            pltpu.VMEM((nslot, rows, LANES), F32),
            pltpu.VMEM((nslot, rows, LANES), F32),
            pltpu.VMEM((rows, 16, LANES), F32),
            pltpu.VMEM((tall, 16, 384), BF16),
            pltpu.VMEM((2, LAYERS, 3, 384, LANES), BF16),
            pltpu.VMEM((LAYERS, rows * 16, LANES), F32),
            pltpu.VMEM((rows, 16, LANES), F32),
            pltpu.VMEM((LANES, 16 * LANES), BF16),
            pltpu.VMEM((9, 16, LANES), F32),
            pltpu.VMEM((ITERS, 9, 16, LANES), F32),
            pltpu.VMEM((ITERS, 9, 16, LANES), F32),
            pltpu.VMEM((ITERS, 9, 16, LANES), F32),
            pltpu.VMEM((144, LANES), F32),
            pltpu.VMEM((ITERS, 16, LANES), F32),
            pltpu.VMEM((ITERS, ndev, 8, LANES), F32),
            pltpu.VMEM((ITERS, 8, LANES), F32),
            pltpu.SemaphoreType.DMA((phases, 9)),
            pltpu.SemaphoreType.DMA((phases, 9)),
            pltpu.SemaphoreType.DMA((ITERS,)),
            pltpu.SemaphoreType.DMA((ITERS,)),
        ],
        compiler_params=pltpu.CompilerParams(
            collective_id=0, has_side_effects=True, vmem_limit_bytes=40 * 1024 * 1024
        ),
    )(dilation, design_t, active_t, film, targ, lanes, wt, blocks, sel, sel.T)
    new_design = new[:, :nparams].T.reshape(nparams, drows, dcols)
    return new_design, obj[:, 1, 0]


def solution(mesh):
    placed = (
        P(None, "rows", "cols"),
        P("rows", "cols"),
        P(),
        P(None, "rows", "cols"),
        P(),
        P(),
        P(),
        P(),
        P(),
        P("rows", "cols"),
        P(),
    )
    return jax.shard_map(
        on_device,
        mesh=mesh,
        in_specs=placed,
        out_specs=(P(None, "rows", "cols"), P()),
        check_vma=False,
    )
```

```python
import functools

import jax
import jax.numpy as jnp
import numpy as np
from jax import lax
from jax.experimental import pallas as pl
from jax.experimental.pallas import tpu as pltpu
from jax.sharding import PartitionSpec as P

DMAX = 8
LAYERS = 4
ITERS = 2
LANES = 128

step_rate = 0.25
norm_eps = 1e-06

MESH = pl.DeviceIdType.MESH
F32 = jnp.float32
BF16 = jnp.bfloat16
OTHERS = [0, 1, 2, 3, 5, 6, 7, 8]
PER_ITER = 2 * LAYERS + 2


def tap_list():
    return [(row_step, col_step) for row_step in (-1, 0, 1) for col_step in (-1, 0, 1)]


def split2(value):
    high = value.astype(BF16)
    return high, (value - high.astype(F32)).astype(BF16)


def kernel(
    cfg,
    dil_ref, design_ref, active_ref, film_ref, target_ref, lanes_ref, wt_ref, blk_ref, sel_ref, selt_ref,
    new_ref, obj_ref,
    edge_t, edge_b, halo_t, halo_b, edge_l, edge_r, halo_l, halo_r,
    side_l, side_r, state_s, xo, xt, xb, wbig, wside, wt_s, pre_s, adj_s, ee_s, bfw, bbk, h_s, hd_s,
    amp9, part, got, grad9, q_s, grad_t, ar1, ar1_src, ar2, ar2_src,
    send_sem, recv_sem, ar_send, ar_recv,
):
    nrow, ncol, rows, total_cells, total_entries = cfg
    nx = rows * 16
    my_r = lax.axis_index("rows")
    my_c = lax.axis_index("cols")

    def exists(m):
        dr, dc = m // 3 - 1, m % 3 - 1
        r, c = my_r + dr, my_c + dc
        return (r >= 0) & (r < nrow) & (c >= 0) & (c < ncol)

    def ident(m):
        dr, dc = m // 3 - 1, m % 3 - 1
        return (my_r + dr, my_c + dc)

    def desc(phase, m, src, dst):
        return pltpu.make_async_remote_copy(
            src_ref=src(m), dst_ref=dst(m),
            send_sem=send_sem.at[phase, m], recv_sem=recv_sem.at[phase, m],
            device_id=ident(m), device_id_type=MESH,
        )

    def start(phase, src, dst):
        for m in OTHERS:
            @pl.when(exists(m))
            def _():
                desc(phase, m, src, dst).start()

    def arrive(phase, src, dst):
        for m in OTHERS:
            @pl.when(exists(8 - m))
            def _():
                desc(phase, m, src, dst).wait_recv()

    def sent(phase, src, dst):
        for m in OTHERS:
            @pl.when(exists(m))
            def _():
                desc(phase, m, src, dst).wait_send()

    def state_refs(slot):
        el, er, hl, hr = edge_l.at[slot], edge_r.at[slot], halo_l.at[slot], halo_r.at[slot]
        D, R = DMAX, rows

        def src(m):
            return {
                0: lambda: el.at[pl.ds(0, D)], 1: lambda: edge_t.at[slot], 2: lambda: er.at[pl.ds(0, D)],
                3: lambda: el, 5: lambda: er,
                6: lambda: el.at[pl.ds(R - D, D)], 7: lambda: edge_b.at[slot], 8: lambda: er.at[pl.ds(R - D, D)],
            }[m]()

        def dst(m):
            return {
                0: lambda: hr.at[pl.ds(R + D, D)], 1: lambda: halo_b.at[slot], 2: lambda: hl.at[pl.ds(R + D, D)],
                3: lambda: hr.at[pl.ds(D, R)], 5: lambda: hl.at[pl.ds(D, R)],
                6: lambda: hr.at[pl.ds(0, D)], 7: lambda: halo_t.at[slot], 8: lambda: hl.at[pl.ds(0, D)],
            }[m]()

        return src, dst

    def amp_refs(_):
        return (lambda m: amp9.at[4]), (lambda m: amp9.at[8 - m])

    def part_refs(it):
        return (lambda m: part.at[it, m]), (lambda m: got.at[it, 8 - m])

    def grad_refs(it):
        return (lambda m: grad_t.at[it]), (lambda m: grad9.at[it, 8 - m])

    nslot = ITERS * 2 * LAYERS
    zt = jnp.zeros((DMAX, 16, LANES), BF16)
    zh = jnp.zeros((rows + 2 * DMAX, LANES), F32)

    def clear(slot, _):
        halo_t[slot] = zt
        halo_b[slot] = zt
        halo_l[slot] = zh
        halo_r[slot] = zh
        return 0

    lax.fori_loop(0, nslot, clear, 0)
    z9 = jnp.zeros((9, 16, LANES), F32)
    amp9[...] = z9
    for it in range(ITERS):
        got[it] = z9
        grad9[it] = z9

    barrier = pltpu.get_barrier_semaphore()

    def greet(r, c):
        pl.semaphore_signal(barrier, inc=1, device_id=(r, c), device_id_type=MESH)

    for k in range(1, ncol):
        greet(my_r, lax.rem(my_c + k, ncol))
    for k in range(1, nrow):
        greet(lax.rem(my_r + k, nrow), my_c)
    greeted = (ncol - 1) + (nrow - 1)
    for m in (0, 2, 6, 8):
        there = exists(m)
        greeted = greeted + jnp.where(there, 1, 0)

        @pl.when(there)
        def _():
            greet(*ident(m))

    x_zero = jnp.zeros((DMAX, 16, 384), BF16)
    xo[0:DMAX] = x_zero
    xo[rows + DMAX : rows + 2 * DMAX] = x_zero
    xt[DMAX : 2 * DMAX] = x_zero
    xb[0:DMAX] = x_zero
    spread_ch = (
        lax.broadcasted_iota(jnp.int32, (16, LANES), 1) % 16 == lax.broadcasted_iota(jnp.int32, (16, LANES), 0)
    ).astype(F32).astype(BF16)
    wt_s[...] = jnp.dot(wt_ref[...], spread_ch, preferred_element_type=F32).reshape(2, LAYERS, 9, 16, LANES)
    pos = lax.broadcasted_iota(jnp.int32, (LANES, 16 * LANES), 0)
    col = lax.broadcasted_iota(jnp.int32, (LANES, 16 * LANES), 1)
    ee_s[...] = (pos == (col // LANES) * 8 + (col % LANES) // 16).astype(F32).astype(BF16)
    for t in range(9):
        b = blk_ref[t]
        bh, bl = split2(b)
        bh, bl = bh.astype(F32), bl.astype(F32)
        bfw[t] = jnp.concatenate([bh, bh, bl], axis=0).astype(BF16)
        bbk[t] = jnp.concatenate([bh, bl, bh], axis=1).astype(BF16)

    amp9[4] = design_ref[...] * active_ref[...]
    new_ref[...] = design_ref[...]
    pl.semaphore_wait(barrier, greeted)
    amp_phase = ITERS * PER_ITER
    start(amp_phase, *amp_refs(0))

    lane = lax.broadcasted_iota(jnp.int32, (24, 16, LANES), 2) // 16
    jpos = lax.broadcasted_iota(jnp.int32, (24, 16, LANES), 0) - 8 - lane
    for l in range(LAYERS):
        d = dil_ref[l]
        masks = [jpos == rx * d for rx in (-1, 0, 1)]
        for f in range(2):
            for ry in range(3):
                acc = jnp.zeros((24, 16, LANES), F32)
                for rx in range(3):
                    acc = jnp.where(masks[rx], wt_s[f, l, 3 * ry + rx][None], acc)
                banded = acc.astype(BF16).reshape(384, LANES)
                wbig[f, l, ry] = banded
                wside[f, l, 0, 128 * ry : 128 * ry + 128] = banded[0:128]
                wside[f, l, 1, 128 * ry : 128 * ry + 128] = banded[256:384]
    ones_block = (
        lax.broadcasted_iota(jnp.int32, (LANES, LANES), 0) // 16
        == lax.broadcasted_iota(jnp.int32, (LANES, LANES), 1) // 16
    ).astype(F32).astype(BF16)

    lw = lanes_ref[0:1, :]
    lb = lanes_ref[1:2, :]
    ro = lanes_ref[2:3, :]

    def shifted(value):
        c0, c1 = value[:, 0:8], value[:, 8:16]
        bs = lax.broadcasted_iota(jnp.int32, c0.shape, 1)
        l0 = jnp.where(bs == 0, 0.0, pltpu.roll(c1, 1, 1))
        r1 = jnp.where(bs == 7, 0.0, pltpu.roll(c0, 7, 1))
        return (
            jnp.concatenate([l0, c0], axis=1).astype(BF16),
            value.astype(BF16),
            jnp.concatenate([c1, r1], axis=1).astype(BF16),
        )

    def conv(slot, phase, f, l, value):
        refs = state_refs(slot)
        v3 = value.reshape(rows, 16, LANES)
        state_s[...] = v3
        edge_t[slot] = v3[0:DMAX].astype(BF16)
        edge_b[slot] = v3[rows - DMAX : rows].astype(BF16)
        edge_l[slot] = state_s[:, 0, :]
        edge_r[slot] = state_s[:, 15, :]
        start(phase, *refs)
        for n, piece in enumerate(shifted(v3)):
            xo[DMAX : rows + DMAX, :, 128 * n : 128 * n + 128] = piece
        d = dil_ref[l]
        out = None
        for ry in range(3):
            lhs = xo[pl.ds(DMAX + (ry - 1) * d, rows)].reshape(nx, 384)
            term = jnp.dot(lhs, wbig[f, l, ry], preferred_element_type=F32)
            out = term if out is None else out + term
        out = out.reshape(rows, 16, LANES)
        arrive(phase, *refs)
        for n, piece in enumerate(shifted(halo_t[slot].astype(F32))):
            xt[0:DMAX, :, 128 * n : 128 * n + 128] = piece
        for n, piece in enumerate(shifted(halo_b[slot].astype(F32))):
            xb[DMAX : 2 * DMAX, :, 128 * n : 128 * n + 128] = piece
        sides = []
        for n, (halo, side) in enumerate(((halo_l, side_l), (halo_r, side_r))):
            side[...] = halo[slot]
            lhs = jnp.concatenate(
                [side[pl.ds(DMAX + (ry - 1) * d, rows), :] for ry in range(3)], axis=1
            ).astype(BF16)
            sides.append(jnp.dot(lhs, wside[f, l, n], preferred_element_type=F32))
        top = jnp.dot(xt[pl.ds(DMAX - d, DMAX)].reshape(16 * DMAX, 384), wbig[f, l, 0], preferred_element_type=F32)
        bot = jnp.dot(xb[pl.ds(d, DMAX)].reshape(16 * DMAX, 384), wbig[f, l, 2], preferred_element_type=F32)
        out = jnp.concatenate(
            [
                out[0:DMAX] + top.reshape(DMAX, 16, LANES),
                out[DMAX : rows - DMAX],
                out[rows - DMAX : rows] + bot.reshape(DMAX, 16, LANES),
            ],
            axis=0,
        )
        bs = lax.broadcasted_iota(jnp.int32, (rows, 8, LANES), 1)
        add0 = jnp.where(bs == 0, sides[0][:, None, :], 0.0)
        add1 = jnp.where(bs == 7, sides[1][:, None, :], 0.0)
        return (out + jnp.concatenate([add0, add1], axis=1)).reshape(nx, LANES)

    def sigmoid(v):
        return 1.0 / (1.0 + jnp.exp(-v))

    def render(amp, dest):
        high, low = split2(amp.reshape(144, LANES))
        high, low = high.astype(F32), low.astype(F32)
        packed = (high + pltpu.roll(low, 16, 1) + pltpu.roll(high, 32, 1)).astype(BF16)
        picked = jnp.dot(sel_ref[...], packed, preferred_element_type=F32).astype(BF16)
        height = None
        for t in range(9):
            term = jnp.dot(picked[16 * t : 16 * t + 16, 0:48], bfw[t], preferred_element_type=F32)
            height = term if height is None else height + term
        two = jnp.concatenate([height[:, 0:128], height[:, 128:256]], axis=0)
        high, low = split2(two)
        spread = jnp.dot(high, ee_s[...], preferred_element_type=F32)
        spread = spread + jnp.dot(low, ee_s[...], preferred_element_type=F32)
        for s in range(2):
            for k in range(16):
                q = 16 * s + k
                y, xh = q // 2, q % 2
                for a in range(rows // 16):
                    dest[16 * a + y, 8 * xh : 8 * xh + 8, :] = spread[
                        16 * s + 8 * a : 16 * s + 8 * a + 8, 128 * k : 128 * k + 128
                    ]

    arrive(amp_phase, *amp_refs(0))
    render(amp9[...], h_s)
    sent(amp_phase, *amp_refs(0))

    def step(it, _):
        base = it * PER_ITER
        slot0 = it * 2 * LAYERS
        h = h_s[...].reshape(nx, LANES)
        state = (lw * h + lb + film_ref[...].astype(F32).reshape(nx, LANES)).astype(BF16).astype(F32)
        for l in range(LAYERS):
            pre = conv(slot0 + l, base + l, 0, l, state) + lanes_ref[4 + l : 5 + l, :]
            pre_s[l] = pre
            state = (state + pre * sigmoid(pre)).astype(BF16).astype(F32)
        pressure = None
        for piece in split2(ro * state):
            term = jnp.dot(piece, ones_block, preferred_element_type=F32)
            pressure = term if pressure is None else pressure + term
        misfit = pressure - target_ref[...].reshape(nx, LANES)
        miss = jnp.sum(misfit * misfit, keepdims=True) * (0.5 / 16)
        adjoint = ro * (misfit * (1.0 / 256.0))
        for n in range(LAYERS):
            l = LAYERS - 1 - n
            v = pre_s[l]
            s = sigmoid(v)
            slope = (adjoint * (s * (1.0 + v * (1.0 - s)))).astype(BF16).astype(F32)
            adjoint = adjoint + conv(slot0 + LAYERS + n, base + LAYERS + n, 1, l, slope)
        adj_s[...] = (lw * adjoint).reshape(rows, 16, LANES)
        strips = []
        for s in range(2):
            tiles = []
            for k in range(16):
                q = 16 * s + k
                y, xh = q // 2, q % 2
                tiles.append(
                    jnp.concatenate(
                        [adj_s[16 * a + y, 8 * xh : 8 * xh + 8, :] for a in range(rows // 16)], axis=0
                    )
                )
            strips.append(jnp.concatenate(tiles, axis=1))
        both = jnp.concatenate(strips, axis=0)
        folded = None
        for piece in split2(both):
            term = lax.dot_general(piece, ee_s[...], (((1,), (1,)), ((), ())), preferred_element_type=F32)
            folded = term if folded is None else folded + term
        hg = jnp.concatenate([folded[0:16], folded[16:32]], axis=1)
        high, low = split2(hg)
        wide = jnp.concatenate([high, high, low], axis=1)
        q_s[...] = jnp.zeros((144, LANES), F32)
        for t in range(9):
            q_s[16 * t : 16 * t + 16, 0:16] = lax.dot_general(
                wide, bbk[t], (((1,), (1,)), ((), ())), preferred_element_type=F32
            )
        mine = None
        for piece in split2(q_s[...]):
            term = jnp.dot(selt_ref[...], piece, preferred_element_type=F32)
            mine = term if mine is None else mine + term
        mine = mine.reshape(9, 16, LANES)
        part[it] = mine
        p_phase = base + 2 * LAYERS
        start(p_phase, *part_refs(it))
        got[it, 4] = mine[4]
        arrive(p_phase, *part_refs(it))
        gradient = jnp.sum(got[it], axis=0) * active_ref[...]
        squares = jnp.sum(gradient * gradient, keepdims=True)
        sub = lax.broadcasted_iota(jnp.int32, (8, LANES), 0)
        tile = jnp.where(sub == 0, squares, miss)
        ar1_src[it] = tile
        g_phase = p_phase + 1

        def ring(n, src, dst, dev):
            return pltpu.make_async_remote_copy(
                src_ref=src.at[it], dst_ref=dst,
                send_sem=ar_send.at[it, n], recv_sem=ar_recv.at[it, n],
                device_id=dev, device_id_type=MESH,
            )

        for k in range(1, ncol):
            ring(0, ar1_src, ar1.at[it, my_c], (my_r, lax.rem(my_c + k, ncol))).start()
        ar1[it, my_c] = tile
        more = it < ITERS - 1

        @pl.when(more)
        def _():
            grad_t[it] = gradient
            start(g_phase, *grad_refs(it))
            grad9[it, 4] = gradient

        many = ar1.at[it, pl.ds(0, ncol - 1)]
        pltpu.make_async_copy(many, many, ar_recv.at[it, 0]).wait()
        tile2 = jnp.sum(ar1[it], axis=0)
        ar2_src[it] = tile2
        for k in range(1, nrow):
            ring(1, ar2_src, ar2.at[it, my_r], (lax.rem(my_r + k, nrow), my_c)).start()
        ar2[it, my_r] = tile2

        @pl.when(more)
        def _():
            arrive(g_phase, *grad_refs(it))
            render(grad9[it], hd_s)

        many = ar2.at[it, pl.ds(0, nrow - 1)]
        pltpu.make_async_copy(many, many, ar_recv.at[it, 1]).wait()
        total = jnp.sum(ar2[it], axis=0)
        scale = step_rate / jnp.sqrt(total[0:1] * (1.0 / total_entries) + norm_eps)
        obj_ref[it] = total * (1.0 / total_cells)
        new_ref[...] = new_ref[...] - gradient * scale

        @pl.when(more)
        def _():
            h_s[...] = h_s[...] - hd_s[...] * scale[None]

        return 0

    lax.fori_loop(0, ITERS, step, 0)

    def drain(it, _):
        base = it * PER_ITER
        for n in range(2 * LAYERS):
            sent(base + n, *state_refs(it * 2 * LAYERS + n))
        sent(base + 2 * LAYERS, *part_refs(it))

        @pl.when(it < ITERS - 1)
        def _():
            sent(base + 2 * LAYERS + 1, *grad_refs(it))

        many = ar1.at[it, pl.ds(0, ncol - 1)]
        pltpu.make_async_copy(many, many, ar_send.at[it, 0]).wait()
        many = ar2.at[it, pl.ds(0, nrow - 1)]
        pltpu.make_async_copy(many, many, ar_send.at[it, 1]).wait()
        return 0

    lax.fori_loop(0, ITERS, drain, 0)


def select_matrix(dr_count, dc_count):
    sel = np.zeros((9, dr_count, dc_count, 9, dr_count, dc_count), np.float32)
    for t, (ry, rx) in enumerate(tap_list()):
        for a in range(dr_count):
            for b in range(dc_count):
                ta, tb = a + ry, b + rx
                nr, nc = ta // dr_count, tb // dc_count
                sel[t, a, b, 3 * (nr + 1) + nc + 1, ta - nr * dr_count, tb - nc * dc_count] = 1
    size = 9 * dr_count * dc_count
    return sel.reshape(size, size)


def basis_blocks(stamp_basis):
    nparams, side = stamp_basis.shape[0], stamp_basis.shape[1] // 2
    half = side // 2
    padded = jnp.pad(stamp_basis, ((0, 16 - nparams), (half, half), (half, half)))
    windows = padded.reshape(16, 3, side, 3, side).transpose(1, 3, 0, 2, 4)
    return windows[::-1, ::-1].reshape(9, 16, side * side)


def on_device(
    design, active, stamp_basis, film_field, lift_weight, lift_bias, conv_weight, conv_bias, readout, target, dilation
):
    channels, rows, cols = film_field.shape
    nparams, drows, dcols = design.shape
    nrow = lax.axis_size("rows")
    ncol = lax.axis_size("cols")
    ndev = nrow * ncol
    total_cells = rows * cols * ndev
    total_entries = nparams * drows * dcols * ndev

    def by_dimple(v):
        v = v.reshape(nparams, drows * dcols).T
        return jnp.pad(v, ((0, 0), (0, LANES - nparams)))

    design_t = by_dimple(design)
    active_t = jnp.broadcast_to(active.astype(F32).reshape(drows * dcols, 1), (drows * dcols, LANES))
    film = film_field.reshape(channels, rows, dcols, 2, 8).transpose(1, 3, 2, 4, 0).reshape(rows, 16, LANES)
    targ = target.reshape(rows, dcols, 2, 8).transpose(0, 2, 1, 3).reshape(rows, 16, 8, 1)
    targ = jnp.broadcast_to(targ, (rows, 16, 8, 16)).reshape(rows, 16, LANES)
    lanes = jnp.concatenate(
        [jnp.tile(jnp.stack([lift_weight, lift_bias, readout, readout]), (1, 8)), jnp.tile(conv_bias, (1, 8))]
    )
    wt = jnp.stack([jnp.swapaxes(conv_weight, 2, 3), conv_weight[:, ::-1]])
    wt = wt.reshape(2 * LAYERS * 9 * channels, channels)
    blocks = basis_blocks(stamp_basis)
    sel = select_matrix(drows, dcols).astype(BF16)

    nslot = ITERS * 2 * LAYERS
    phases = ITERS * PER_ITER + 1
    tall = rows + 2 * DMAX
    vmem = pl.BlockSpec(memory_space=pltpu.VMEM)
    new, obj = pl.pallas_call(
        functools.partial(kernel, (nrow, ncol, rows, total_cells, total_entries)),
        out_shape=(
            jax.ShapeDtypeStruct((16, LANES), F32),
            jax.ShapeDtypeStruct((ITERS, 8, LANES), F32),
        ),
        in_specs=[pl.BlockSpec(memory_space=pltpu.SMEM)] + [vmem] * 9,
        out_specs=(vmem, vmem),
        scratch_shapes=[
            pltpu.VMEM((nslot, DMAX, 16, LANES), BF16),
            pltpu.VMEM((nslot, DMAX, 16, LANES), BF16),
            pltpu.VMEM((nslot, DMAX, 16, LANES), BF16),
            pltpu.VMEM((nslot, DMAX, 16, LANES), BF16),
            pltpu.VMEM((nslot, rows, LANES), F32),
            pltpu.VMEM((nslot, rows, LANES), F32),
            pltpu.VMEM((nslot, tall, LANES), F32),
            pltpu.VMEM((nslot, tall, LANES), F32),
            pltpu.VMEM((tall, LANES), F32),
            pltpu.VMEM((tall, LANES), F32),
            pltpu.VMEM((rows, 16, LANES), F32),
            pltpu.VMEM((tall, 16, 384), BF16),
            pltpu.VMEM((2 * DMAX, 16, 384), BF16),
            pltpu.VMEM((2 * DMAX, 16, 384), BF16),
            pltpu.VMEM((2, LAYERS, 3, 384, LANES), BF16),
            pltpu.VMEM((2, LAYERS, 2, 384, LANES), BF16),
            pltpu.VMEM((2, LAYERS, 9, 16, LANES), F32),
            pltpu.VMEM((LAYERS, rows * 16, LANES), F32),
            pltpu.VMEM((rows, 16, LANES), F32),
            pltpu.VMEM((LANES, 16 * LANES), BF16),
            pltpu.VMEM((9, 48, 256), BF16),
            pltpu.VMEM((9, 16, 768), BF16),
            pltpu.VMEM((rows, 16, LANES), F32),
            pltpu.VMEM((rows, 16, LANES), F32),
            pltpu.VMEM((9, 16, LANES), F32),
            pltpu.VMEM((ITERS, 9, 16, LANES), F32),
            pltpu.VMEM((ITERS, 9, 16, LANES), F32),
            pltpu.VMEM((ITERS, 9, 16, LANES), F32),
            pltpu.VMEM((144, LANES), F32),
            pltpu.VMEM((ITERS, 16, LANES), F32),
            pltpu.VMEM((ITERS, ncol, 8, LANES), F32),
            pltpu.VMEM((ITERS, 8, LANES), F32),
            pltpu.VMEM((ITERS, nrow, 8, LANES), F32),
            pltpu.VMEM((ITERS, 8, LANES), F32),
            pltpu.SemaphoreType.DMA((phases, 9)),
            pltpu.SemaphoreType.DMA((phases, 9)),
            pltpu.SemaphoreType.DMA((ITERS, 2)),
            pltpu.SemaphoreType.DMA((ITERS, 2)),
        ],
        compiler_params=pltpu.CompilerParams(
            collective_id=0, has_side_effects=True, vmem_limit_bytes=40 * 1024 * 1024
        ),
    )(dilation, design_t, active_t, film, targ, lanes, wt, blocks, sel, sel.T)
    new_design = new[:, :nparams].T.reshape(nparams, drows, dcols)
    return new_design, obj[:, 1, 0]


def solution(mesh):
    placed = (
        P(None, "rows", "cols"),
        P("rows", "cols"),
        P(),
        P(None, "rows", "cols"),
        P(),
        P(),
        P(),
        P(),
        P(),
        P("rows", "cols"),
        P(),
    )
    return jax.shard_map(
        on_device,
        mesh=mesh,
        in_specs=placed,
        out_specs=(P(None, "rows", "cols"), P()),
        check_vma=False,
    )
```

```python
import functools

import jax
import jax.numpy as jnp
import numpy as np
from jax import lax
from jax.experimental import pallas as pl
from jax.experimental.pallas import tpu as pltpu
from jax.sharding import PartitionSpec as P

DMAX = 8
LAYERS = 4
ITERS = 2
LANES = 128

step_rate = 0.25
norm_eps = 1e-06

MESH = pl.DeviceIdType.MESH
F32 = jnp.float32
BF16 = jnp.bfloat16
OTHERS = [0, 1, 2, 3, 5, 6, 7, 8]
PAIRS = LAYERS // 2
PER_ITER = 2 * PAIRS + 2
HALO = 2 * DMAX


def tap_list():
    return [(row_step, col_step) for row_step in (-1, 0, 1) for col_step in (-1, 0, 1)]


def split2(value):
    high = value.astype(BF16)
    return high, (value - high.astype(F32)).astype(BF16)


def kernel(
    cfg,
    dil_ref, design_ref, active_ref, film_ref, target_ref, lanes_ref, wt_ref, blk_ref, sel_ref, selt_ref,
    new_ref, obj_ref,
    edge_t, edge_b, halo_t, halo_b, edge_l, edge_r, halo_l, halo_r,
    cf_s, side_s, xo, xn, wbig, wside, wt_s, pre_o, pre_c, pre_w, adj_s, ee_s, bfw, bbk, h_s, hd_s,
    amp9, part, got, grad9, q_s, grad_t, ar1, ar1_src, ar2, ar2_src,
    send_sem, recv_sem, ar_send, ar_recv,
):
    nrow, ncol, rows, total_cells, total_entries = cfg
    nx = rows * 16
    my_r = lax.axis_index("rows")
    my_c = lax.axis_index("cols")

    def exists(m):
        dr, dc = m // 3 - 1, m % 3 - 1
        r, c = my_r + dr, my_c + dc
        return (r >= 0) & (r < nrow) & (c >= 0) & (c < ncol)

    def ident(m):
        dr, dc = m // 3 - 1, m % 3 - 1
        return (my_r + dr, my_c + dc)

    def desc(phase, m, src, dst):
        return pltpu.make_async_remote_copy(
            src_ref=src(m), dst_ref=dst(m),
            send_sem=send_sem.at[phase, m], recv_sem=recv_sem.at[phase, m],
            device_id=ident(m), device_id_type=MESH,
        )

    def start(phase, src, dst):
        for m in OTHERS:
            @pl.when(exists(m))
            def _():
                desc(phase, m, src, dst).start()

    def arrive(phase, src, dst):
        for m in OTHERS:
            @pl.when(exists(8 - m))
            def _():
                desc(phase, m, src, dst).wait_recv()

    def sent(phase, src, dst):
        for m in OTHERS:
            @pl.when(exists(m))
            def _():
                desc(phase, m, src, dst).wait_send()

    def state_refs(slot, both):
        n, g = (HALO + DMAX, 3) if both else (HALO, 2)
        H, R = HALO, rows
        el, er, hl, hr = [ref.at[slot, pl.ds(0, g)] for ref in (edge_l, edge_r, halo_l, halo_r)]
        et, eb, ht, hb = [ref.at[slot, pl.ds(0, n)] for ref in (edge_t, edge_b, halo_t, halo_b)]

        def cut(ref, at, size):
            return ref.at[:, pl.ds(at, size)]

        def src(m):
            return {
                0: lambda: cut(el, 0, H), 1: lambda: et, 2: lambda: cut(er, 0, H),
                3: lambda: el, 5: lambda: er,
                6: lambda: cut(el, R - H, H), 7: lambda: eb, 8: lambda: cut(er, R - H, H),
            }[m]()

        def dst(m):
            return {
                0: lambda: cut(hr, R + H, H), 1: lambda: hb, 2: lambda: cut(hl, R + H, H),
                3: lambda: cut(hr, H, R), 5: lambda: cut(hl, H, R),
                6: lambda: cut(hr, 0, H), 7: lambda: ht, 8: lambda: cut(hl, 0, H),
            }[m]()

        return src, dst

    def amp_refs(_):
        return (lambda m: amp9.at[4]), (lambda m: amp9.at[8 - m])

    def part_refs(it):
        return (lambda m: part.at[it, m]), (lambda m: got.at[it, 8 - m])

    def grad_refs(it):
        return (lambda m: grad_t.at[it]), (lambda m: grad9.at[it, 8 - m])

    nslot = ITERS * 2 * PAIRS
    zt = jnp.zeros((HALO + DMAX, 16, LANES), BF16)
    zh = jnp.zeros((3, rows + 2 * HALO, LANES), BF16)

    def clear(slot, _):
        halo_t[slot] = zt
        halo_b[slot] = zt
        halo_l[slot] = zh
        halo_r[slot] = zh
        return 0

    lax.fori_loop(0, nslot, clear, 0)
    z9 = jnp.zeros((9, 16, LANES), F32)
    amp9[...] = z9
    for it in range(ITERS):
        got[it] = z9
        grad9[it] = z9

    barrier = pltpu.get_barrier_semaphore()

    def greet(r, c):
        pl.semaphore_signal(barrier, inc=1, device_id=(r, c), device_id_type=MESH)

    for k in range(1, ncol):
        greet(my_r, lax.rem(my_c + k, ncol))
    for k in range(1, nrow):
        greet(lax.rem(my_r + k, nrow), my_c)
    greeted = (ncol - 1) + (nrow - 1)
    for m in (0, 2, 6, 8):
        there = exists(m)
        greeted = greeted + jnp.where(there, 1, 0)

        @pl.when(there)
        def _():
            greet(*ident(m))

    spread_ch = (
        lax.broadcasted_iota(jnp.int32, (16, LANES), 1) % 16 == lax.broadcasted_iota(jnp.int32, (16, LANES), 0)
    ).astype(F32).astype(BF16)
    wt_s[...] = jnp.dot(wt_ref[...], spread_ch, preferred_element_type=F32).reshape(2, LAYERS, 9, 16, LANES)
    pos = lax.broadcasted_iota(jnp.int32, (LANES, 16 * LANES), 0)
    col = lax.broadcasted_iota(jnp.int32, (LANES, 16 * LANES), 1)
    ee_s[...] = (pos == (col // LANES) * 8 + (col % LANES) // 16).astype(F32).astype(BF16)
    for t in range(9):
        b = blk_ref[8 - t]
        bh, bl = split2(b)
        bh, bl = bh.astype(F32), bl.astype(F32)
        bfw[t] = jnp.concatenate([bh, bh, bl], axis=0).astype(BF16)
        bbk[t] = jnp.concatenate([bh, bl, bh], axis=1).astype(BF16)

    amp9[4] = design_ref[...] * active_ref[...]
    new_ref[...] = design_ref[...]
    pl.semaphore_wait(barrier, greeted)
    amp_phase = ITERS * PER_ITER
    start(amp_phase, *amp_refs(0))

    lane = lax.broadcasted_iota(jnp.int32, (24, 16, LANES), 2) // 16
    jpos = lax.broadcasted_iota(jnp.int32, (24, 16, LANES), 0) - 8 - lane
    for l in range(LAYERS):
        d = dil_ref[l]
        masks = [jpos == rx * d for rx in (-1, 0, 1)]
        for f in range(2):
            for ry in range(3):
                acc = jnp.zeros((24, 16, LANES), F32)
                for rx in range(3):
                    acc = jnp.where(masks[rx], wt_s[f, l, 3 * ry + rx][None], acc)
                banded = acc.astype(BF16).reshape(384, LANES)
                wbig[f, l, ry] = banded
                wside[f, l, 0, 128 * ry : 128 * ry + 128] = banded[0:128]
                wside[f, l, 1, 128 * ry : 128 * ry + 128] = banded[256:384]
    ones_block = (
        lax.broadcasted_iota(jnp.int32, (LANES, LANES), 0) // 16
        == lax.broadcasted_iota(jnp.int32, (LANES, LANES), 1) // 16
    ).astype(F32).astype(BF16)

    lw = lanes_ref[0:1, :]
    lb = lanes_ref[1:2, :]
    ro = lanes_ref[2:3, :]

    def shifted(value, left=None, right=None):
        c0, c1 = value[:, 0:8], value[:, 8:16]
        bs = lax.broadcasted_iota(jnp.int32, c0.shape, 1)
        l0 = jnp.where(bs == 0, 0.0 if left is None else left[:, None, :], pltpu.roll(c1, 1, 1))
        r1 = jnp.where(bs == 7, 0.0 if right is None else right[:, None, :], pltpu.roll(c0, 7, 1))
        return (
            jnp.concatenate([l0, c0], axis=1).astype(BF16),
            value.astype(BF16),
            jnp.concatenate([c1, r1], axis=1).astype(BF16),
        )

    def put(ref, at, pieces):
        for n, piece in enumerate(pieces):
            ref[at : at + piece.shape[0], :, 128 * n : 128 * n + 128] = piece

    def conv_rows(ref, f, l, at, count):
        d = dil_ref[l]
        out = None
        for ry in range(3):
            lhs = ref[pl.ds(at + (ry - 1) * d, count)].reshape(16 * count, 384)
            term = jnp.dot(lhs, wbig[f, l, ry], preferred_element_type=F32)
            out = term if out is None else out + term
        return out.reshape(count, 16, LANES)

    def f32(value):
        return value.astype(F32)

    tall = rows + 2 * DMAX

    def wide_conv(slot, phase, f, l, v3, extra=None):
        H, D, R = HALO, DMAX, rows
        refs = state_refs(slot, extra is not None)
        cf_s[H : H + R] = v3
        edge_t[slot, 0:H] = v3[0:H].astype(BF16)
        edge_b[slot, 0:H] = v3[R - H : R].astype(BF16)
        for n, (gl, gr) in enumerate(((0, 15), (8, 7))):
            edge_l[slot, n] = cf_s[H : H + R, gl, :].astype(BF16)
            edge_r[slot, n] = cf_s[H : H + R, gr, :].astype(BF16)
        if extra is not None:
            adj_s[...] = extra
            edge_t[slot, H : H + D] = extra[0:D].astype(BF16)
            edge_b[slot, H : H + D] = extra[R - D : R].astype(BF16)
            edge_l[slot, 2] = adj_s[:, 0, :].astype(BF16)
            edge_r[slot, 2] = adj_s[:, 15, :].astype(BF16)
        start(phase, *refs)
        put(xo, H, shifted(v3))
        mid = conv_rows(xo, f, l, H + D, R - 2 * D)
        arrive(phase, *refs)
        above, below = f32(halo_t[slot, 0:H]), f32(halo_b[slot, 0:H])
        cf_s[0:H] = above
        cf_s[H + R : 2 * H + R] = below
        put(xo, 0, shifted(above))
        put(xo, H + R, shifted(below))
        top = conv_rows(xo, f, l, H - D, 2 * D)
        bot = conv_rows(xo, f, l, H + R - D, 2 * D)
        side_s[0] = f32(halo_l[slot, 1])
        side_s[1] = f32(halo_l[slot, 0])
        side_s[2] = cf_s[:, 0, :]
        side_s[3] = cf_s[:, 15, :]
        side_s[4] = f32(halo_r[slot, 0])
        side_s[5] = f32(halo_r[slot, 1])
        d = dil_ref[l]
        outer = None
        near = ([], [])
        for ry in range(3):
            six = [side_s[n, pl.ds(H - D + (ry - 1) * d, tall), :] for n in range(6)]
            for n in range(2):
                near[n].append(six[3 * n + 1])
            lhs = jnp.concatenate(
                [jnp.concatenate(six[0:3], axis=1), jnp.concatenate(six[3:6], axis=1)], axis=0
            ).astype(BF16)
            term = jnp.dot(lhs, wbig[f, l, ry], preferred_element_type=F32)
            outer = term if outer is None else outer + term
        inner = [
            jnp.dot(
                jnp.concatenate(near[n], axis=1).astype(BF16), wside[f, l, n], preferred_element_type=F32
            )
            for n in range(2)
        ]
        bs = lax.broadcasted_iota(jnp.int32, (tall, 8, LANES), 1)
        add0 = jnp.where(bs == 0, inner[0][:, None, :], 0.0)
        add1 = jnp.where(bs == 7, inner[1][:, None, :], 0.0)
        out = jnp.concatenate([top, mid, bot], axis=0) + jnp.concatenate([add0, add1], axis=1)
        return out, outer[0:tall], outer[tall : 2 * tall]

    inside = [jnp.where(exists(m), 1.0, 0.0).astype(F32) for m in (1, 7, 3, 5)]

    def clip_map(value):
        D, R = DMAX, rows
        return jnp.concatenate(
            [value[0:D] * inside[0], value[D : D + R], value[D + R : 2 * D + R] * inside[1]], axis=0
        )

    def near_conv(f, l, c3, left, right):
        put(xn, 0, shifted(clip_map(c3), clip_map(left) * inside[2], clip_map(right) * inside[3]))
        return conv_rows(xn, f, l, DMAX, rows)

    def sigmoid(v):
        return 1.0 / (1.0 + jnp.exp(-v))

    def render(amp, dest):
        high, low = split2(amp.reshape(144, LANES))
        high, low = high.astype(F32), low.astype(F32)
        packed = (high + pltpu.roll(low, 16, 1) + pltpu.roll(high, 32, 1)).astype(BF16)
        picked = jnp.dot(sel_ref[...], packed, preferred_element_type=F32).astype(BF16)
        height = None
        for t in range(9):
            term = jnp.dot(picked[16 * t : 16 * t + 16, 0:48], bfw[t], preferred_element_type=F32)
            height = term if height is None else height + term
        two = jnp.concatenate([height[:, 0:128], height[:, 128:256]], axis=0)
        high, low = split2(two)
        spread = jnp.dot(high, ee_s[...], preferred_element_type=F32)
        spread = spread + jnp.dot(low, ee_s[...], preferred_element_type=F32)
        for s in range(2):
            for k in range(16):
                q = 16 * s + k
                y, xh = q // 2, q % 2
                for a in range(rows // 16):
                    dest[16 * a + y, 8 * xh : 8 * xh + 8, :] = spread[
                        16 * s + 8 * a : 16 * s + 8 * a + 8, 128 * k : 128 * k + 128
                    ]

    arrive(amp_phase, *amp_refs(0))
    render(amp9[...], h_s)
    sent(amp_phase, *amp_refs(0))

    def step(it, _):
        base = it * PER_ITER
        slot0 = it * 2 * PAIRS
        D, R = DMAX, rows
        state = f32((lw * h_s[...] + lb + f32(film_ref[...])).astype(BF16))
        for n in range(PAIRS):
            la, lb_ = 2 * n, 2 * n + 1
            bias = lanes_ref[4 + la : 5 + la, :]
            outs = wide_conv(slot0 + n, base + n, 0, la, state)
            olds = (cf_s[D : D + tall], side_s[1, D : D + tall], side_s[4, D : D + tall])
            news = []
            for k in range(3):
                pre = outs[k] + bias
                if k == 0:
                    pre_c[n] = pre
                else:
                    pre_w[n, k - 1] = pre
                news.append(f32((olds[k] + pre * sigmoid(pre)).astype(BF16)))
            pre = near_conv(0, lb_, *news) + lanes_ref[4 + lb_ : 5 + lb_, :]
            pre_o[n] = pre
            state = f32((news[0][D : D + R] + pre * sigmoid(pre)).astype(BF16))
        pressure = None
        for piece in split2((ro * state).reshape(nx, LANES)):
            term = jnp.dot(piece, ones_block, preferred_element_type=F32)
            pressure = term if pressure is None else pressure + term
        misfit = pressure - target_ref[...].reshape(nx, LANES)
        miss = jnp.sum(misfit * misfit, keepdims=True) * (0.5 / 16)
        adjoint = (ro * (misfit * (1.0 / 256.0))).reshape(rows, 16, LANES)

        def slope_of(grad, v):
            s = sigmoid(v)
            return f32((grad * (s * (1.0 + v * (1.0 - s)))).astype(BF16))

        for n in range(PAIRS):
            pair = PAIRS - 1 - n
            slot = slot0 + PAIRS + n
            slope = slope_of(adjoint, pre_o[pair])
            outs = wide_conv(slot, base + PAIRS + n, 1, 2 * pair + 1, slope, adjoint)
            grown = jnp.concatenate(
                [f32(halo_t[slot, HALO : HALO + D]), adjoint, f32(halo_b[slot, HALO : HALO + D])], axis=0
            )
            adjs = (
                grown + outs[0],
                f32(halo_l[slot, 2])[D : D + tall] + outs[1],
                f32(halo_r[slot, 2])[D : D + tall] + outs[2],
            )
            pres = (pre_c[pair], pre_w[pair, 0], pre_w[pair, 1])
            slopes = [slope_of(x, v) for x, v in zip(adjs, pres)]
            adjoint = adjs[0][D : D + R] + near_conv(1, 2 * pair, *slopes)
        adj_s[...] = lw * adjoint
        strips = []
        for s in range(2):
            tiles = []
            for k in range(16):
                q = 16 * s + k
                y, xh = q // 2, q % 2
                tiles.append(
                    jnp.concatenate(
                        [adj_s[16 * a + y, 8 * xh : 8 * xh + 8, :] for a in range(rows // 16)], axis=0
                    )
                )
            strips.append(jnp.concatenate(tiles, axis=1))
        both = jnp.concatenate(strips, axis=0)
        folded = None
        for piece in split2(both):
            term = lax.dot_general(piece, ee_s[...], (((1,), (1,)), ((), ())), preferred_element_type=F32)
            folded = term if folded is None else folded + term
        hg = jnp.concatenate([folded[0:16], folded[16:32]], axis=1)
        high, low = split2(hg)
        wide = jnp.concatenate([high, high, low], axis=1)
        q_s[...] = jnp.zeros((144, LANES), F32)
        for t in range(9):
            q_s[16 * t : 16 * t + 16, 0:16] = lax.dot_general(
                wide, bbk[t], (((1,), (1,)), ((), ())), preferred_element_type=F32
            )
        mine = None
        for piece in split2(q_s[...]):
            term = jnp.dot(selt_ref[...], piece, preferred_element_type=F32)
            mine = term if mine is None else mine + term
        mine = mine.reshape(9, 16, LANES)
        part[it] = mine
        p_phase = base + 2 * PAIRS
        start(p_phase, *part_refs(it))
        got[it, 4] = mine[4]
        arrive(p_phase, *part_refs(it))
        gradient = jnp.sum(got[it], axis=0) * active_ref[...]
        squares = jnp.sum(gradient * gradient, keepdims=True)
        sub = lax.broadcasted_iota(jnp.int32, (8, LANES), 0)
        tile = jnp.where(sub == 0, squares, miss)
        ar1_src[it] = tile
        g_phase = p_phase + 1

        def ring(n, src, dst, dev):
            return pltpu.make_async_remote_copy(
                src_ref=src.at[it], dst_ref=dst,
                send_sem=ar_send.at[it, n], recv_sem=ar_recv.at[it, n],
                device_id=dev, device_id_type=MESH,
            )

        for k in range(1, ncol):
            ring(0, ar1_src, ar1.at[it, my_c], (my_r, lax.rem(my_c + k, ncol))).start()
        ar1[it, my_c] = tile
        more = it < ITERS - 1

        @pl.when(more)
        def _():
            grad_t[it] = gradient
            start(g_phase, *grad_refs(it))
            grad9[it, 4] = gradient

        many = ar1.at[it, pl.ds(0, ncol - 1)]
        pltpu.make_async_copy(many, many, ar_recv.at[it, 0]).wait()
        tile2 = jnp.sum(ar1[it], axis=0)
        ar2_src[it] = tile2
        for k in range(1, nrow):
            ring(1, ar2_src, ar2.at[it, my_r], (lax.rem(my_r + k, nrow), my_c)).start()
        ar2[it, my_r] = tile2

        @pl.when(more)
        def _():
            arrive(g_phase, *grad_refs(it))
            render(grad9[it], hd_s)

        many = ar2.at[it, pl.ds(0, nrow - 1)]
        pltpu.make_async_copy(many, many, ar_recv.at[it, 1]).wait()
        total = jnp.sum(ar2[it], axis=0)
        scale = step_rate / jnp.sqrt(total[0:1] * (1.0 / total_entries) + norm_eps)
        obj_ref[it] = total * (1.0 / total_cells)
        new_ref[...] = new_ref[...] - gradient * scale

        @pl.when(more)
        def _():
            h_s[...] = h_s[...] - hd_s[...] * scale[None]

        return 0

    lax.fori_loop(0, ITERS, step, 0)

    def drain(it, _):
        base = it * PER_ITER
        for n in range(2 * PAIRS):
            sent(base + n, *state_refs(it * 2 * PAIRS + n, n >= PAIRS))
        sent(base + 2 * PAIRS, *part_refs(it))

        @pl.when(it < ITERS - 1)
        def _():
            sent(base + 2 * PAIRS + 1, *grad_refs(it))

        many = ar1.at[it, pl.ds(0, ncol - 1)]
        pltpu.make_async_copy(many, many, ar_send.at[it, 0]).wait()
        many = ar2.at[it, pl.ds(0, nrow - 1)]
        pltpu.make_async_copy(many, many, ar_send.at[it, 1]).wait()
        return 0

    lax.fori_loop(0, ITERS, drain, 0)


def select_matrix(dr_count, dc_count):
    sel = np.zeros((9, dr_count, dc_count, 9, dr_count, dc_count), np.float32)
    for t, (ry, rx) in enumerate(tap_list()):
        for a in range(dr_count):
            for b in range(dc_count):
                ta, tb = a + ry, b + rx
                nr, nc = ta // dr_count, tb // dc_count
                sel[t, a, b, 3 * (nr + 1) + nc + 1, ta - nr * dr_count, tb - nc * dc_count] = 1
    size = 9 * dr_count * dc_count
    return sel.reshape(size, size)


def basis_blocks(stamp_basis):
    nparams, side = stamp_basis.shape[0], stamp_basis.shape[1] // 2
    half = side // 2
    padded = jnp.pad(stamp_basis, ((0, 16 - nparams), (half, half), (half, half)))
    windows = padded.reshape(16, 3, side, 3, side).transpose(1, 3, 0, 2, 4)
    return windows.reshape(9, 16, side * side)


def on_device(
    design, active, stamp_basis, film_field, lift_weight, lift_bias, conv_weight, conv_bias, readout, target, dilation
):
    channels, rows, cols = film_field.shape
    nparams, drows, dcols = design.shape
    nrow = lax.axis_size("rows")
    ncol = lax.axis_size("cols")
    ndev = nrow * ncol
    total_cells = rows * cols * ndev
    total_entries = nparams * drows * dcols * ndev

    def by_dimple(v):
        v = v.reshape(nparams, drows * dcols).T
        return jnp.pad(v, ((0, 0), (0, LANES - nparams)))

    design_t = by_dimple(design)
    active_t = jnp.broadcast_to(active.astype(F32).reshape(drows * dcols, 1), (drows * dcols, LANES))
    film = film_field.reshape(channels, rows, dcols, 2, 8).transpose(1, 3, 2, 4, 0).reshape(rows, 16, LANES)
    targ = target.reshape(rows, dcols, 2, 8).transpose(0, 2, 1, 3).reshape(rows, 16, 8, 1)
    targ = jnp.broadcast_to(targ, (rows, 16, 8, 16)).reshape(rows, 16, LANES)
    lanes = jnp.concatenate(
        [jnp.tile(jnp.stack([lift_weight, lift_bias, readout, readout]), (1, 8)), jnp.tile(conv_bias, (1, 8))]
    )
    wt = jnp.stack([jnp.swapaxes(conv_weight, 2, 3), conv_weight[:, ::-1]])
    wt = wt.reshape(2 * LAYERS * 9 * channels, channels)
    blocks = basis_blocks(stamp_basis)
    sel = select_matrix(drows, dcols).astype(BF16)

    nslot = ITERS * 2 * PAIRS
    phases = ITERS * PER_ITER + 1
    tall = rows + 2 * DMAX
    vmem = pl.BlockSpec(memory_space=pltpu.VMEM)
    new, obj = pl.pallas_call(
        functools.partial(kernel, (nrow, ncol, rows, total_cells, total_entries)),
        out_shape=(
            jax.ShapeDtypeStruct((16, LANES), F32),
            jax.ShapeDtypeStruct((ITERS, 8, LANES), F32),
        ),
        in_specs=[pl.BlockSpec(memory_space=pltpu.SMEM)] + [vmem] * 9,
        out_specs=(vmem, vmem),
        scratch_shapes=[
            pltpu.VMEM((nslot, HALO + DMAX, 16, LANES), BF16),
            pltpu.VMEM((nslot, HALO + DMAX, 16, LANES), BF16),
            pltpu.VMEM((nslot, HALO + DMAX, 16, LANES), BF16),
            pltpu.VMEM((nslot, HALO + DMAX, 16, LANES), BF16),
            pltpu.VMEM((nslot, 3, rows, LANES), BF16),
            pltpu.VMEM((nslot, 3, rows, LANES), BF16),
            pltpu.VMEM((nslot, 3, rows + 2 * HALO, LANES), BF16),
            pltpu.VMEM((nslot, 3, rows + 2 * HALO, LANES), BF16),
            pltpu.VMEM((rows + 2 * HALO, 16, LANES), F32),
            pltpu.VMEM((6, rows + 2 * HALO, LANES), F32),
            pltpu.VMEM((rows + 2 * HALO, 16, 384), BF16),
            pltpu.VMEM((tall, 16, 384), BF16),
            pltpu.VMEM((2, LAYERS, 3, 384, LANES), BF16),
            pltpu.VMEM((2, LAYERS, 2, 384, LANES), BF16),
            pltpu.VMEM((2, LAYERS, 9, 16, LANES), F32),
            pltpu.VMEM((PAIRS, rows, 16, LANES), F32),
            pltpu.VMEM((PAIRS, tall, 16, LANES), F32),
            pltpu.VMEM((PAIRS, 2, tall, LANES), F32),
            pltpu.VMEM((rows, 16, LANES), F32),
            pltpu.VMEM((LANES, 16 * LANES), BF16),
            pltpu.VMEM((9, 48, 256), BF16),
            pltpu.VMEM((9, 16, 768), BF16),
            pltpu.VMEM((rows, 16, LANES), F32),
            pltpu.VMEM((rows, 16, LANES), F32),
            pltpu.VMEM((9, 16, LANES), F32),
            pltpu.VMEM((ITERS, 9, 16, LANES), F32),
            pltpu.VMEM((ITERS, 9, 16, LANES), F32),
            pltpu.VMEM((ITERS, 9, 16, LANES), F32),
            pltpu.VMEM((144, LANES), F32),
            pltpu.VMEM((ITERS, 16, LANES), F32),
            pltpu.VMEM((ITERS, ncol, 8, LANES), F32),
            pltpu.VMEM((ITERS, 8, LANES), F32),
            pltpu.VMEM((ITERS, nrow, 8, LANES), F32),
            pltpu.VMEM((ITERS, 8, LANES), F32),
            pltpu.SemaphoreType.DMA((phases, 9)),
            pltpu.SemaphoreType.DMA((phases, 9)),
            pltpu.SemaphoreType.DMA((ITERS, 2)),
            pltpu.SemaphoreType.DMA((ITERS, 2)),
        ],
        compiler_params=pltpu.CompilerParams(
            collective_id=0, has_side_effects=True, vmem_limit_bytes=40 * 1024 * 1024
        ),
    )(dilation, design_t, active_t, film, targ, lanes, wt, blocks, sel, sel.T)
    new_design = new[:, :nparams].T.reshape(nparams, drows, dcols)
    return new_design, obj[:, 1, 0]


def solution(mesh):
    placed = (
        P(None, "rows", "cols"),
        P("rows", "cols"),
        P(),
        P(None, "rows", "cols"),
        P(),
        P(),
        P(),
        P(),
        P(),
        P("rows", "cols"),
        P(),
    )
    return jax.shard_map(
        on_device,
        mesh=mesh,
        in_specs=placed,
        out_specs=(P(None, "rows", "cols"), P()),
        check_vma=False,
    )
```

```python
import functools

import jax
import jax.numpy as jnp
import numpy as np
from jax import lax
from jax.experimental import pallas as pl
from jax.experimental.pallas import tpu as pltpu
from jax.sharding import PartitionSpec as P

DMAX = 8
LAYERS = 4
ITERS = 2
LANES = 128

step_rate = 0.25
norm_eps = 1e-06

MESH = pl.DeviceIdType.MESH
F32 = jnp.float32
BF16 = jnp.bfloat16
OTHERS = [0, 1, 2, 3, 5, 6, 7, 8]
PAIRS = LAYERS // 2
PER_ITER = 2 * PAIRS + 2
HALO = 2 * DMAX


def tap_list():
    return [(row_step, col_step) for row_step in (-1, 0, 1) for col_step in (-1, 0, 1)]


def split2(value):
    high = value.astype(BF16)
    return high, (value - high.astype(F32)).astype(BF16)


def kernel(
    cfg,
    dil_ref, design_ref, active_ref, film_ref, target_ref, lanes_ref, wt_ref, blk_ref, sel_ref, selt_ref,
    new_ref, obj_ref,
    edge_t, edge_b, halo_t, halo_b, edge_l, edge_r, halo_l, halo_r,
    cf_s, side_s, xo, xn, wbig, wside, wt_s, steep_o, steep_c, steep_w, adj_s, ee_s, bfw, bbk, h_s, hd_s,
    amp9, part, got, grad9, q_s, grad_t, ar1, ar1_src, ar2, ar2_src,
    send_sem, recv_sem, ar_send, ar_recv,
):
    nrow, ncol, rows, total_cells, total_entries = cfg
    nx = rows * 16
    my_r = lax.axis_index("rows")
    my_c = lax.axis_index("cols")

    def exists(m):
        dr, dc = m // 3 - 1, m % 3 - 1
        r, c = my_r + dr, my_c + dc
        return (r >= 0) & (r < nrow) & (c >= 0) & (c < ncol)

    def ident(m):
        dr, dc = m // 3 - 1, m % 3 - 1
        return (my_r + dr, my_c + dc)

    def desc(phase, m, src, dst):
        return pltpu.make_async_remote_copy(
            src_ref=src(m), dst_ref=dst(m),
            send_sem=send_sem.at[phase, m], recv_sem=recv_sem.at[phase, m],
            device_id=ident(m), device_id_type=MESH,
        )

    def start(phase, src, dst):
        for m in OTHERS:
            @pl.when(exists(m))
            def _():
                desc(phase, m, src, dst).start()

    def arrive(phase, src, dst):
        for m in OTHERS:
            @pl.when(exists(8 - m))
            def _():
                desc(phase, m, src, dst).wait_recv()

    def sent(phase, src, dst):
        for m in OTHERS:
            @pl.when(exists(m))
            def _():
                desc(phase, m, src, dst).wait_send()

    def state_refs(slot, both):
        n, g = (HALO + DMAX, 3) if both else (HALO, 2)
        H, R = HALO, rows
        el, er, hl, hr = [ref.at[slot, pl.ds(0, g)] for ref in (edge_l, edge_r, halo_l, halo_r)]
        et, eb, ht, hb = [ref.at[slot, pl.ds(0, n)] for ref in (edge_t, edge_b, halo_t, halo_b)]

        def cut(ref, at, size):
            return ref.at[:, pl.ds(at, size)]

        def src(m):
            return {
                0: lambda: cut(el, 0, H), 1: lambda: et, 2: lambda: cut(er, 0, H),
                3: lambda: el, 5: lambda: er,
                6: lambda: cut(el, R - H, H), 7: lambda: eb, 8: lambda: cut(er, R - H, H),
            }[m]()

        def dst(m):
            return {
                0: lambda: cut(hr, R + H, H), 1: lambda: hb, 2: lambda: cut(hl, R + H, H),
                3: lambda: cut(hr, H, R), 5: lambda: cut(hl, H, R),
                6: lambda: cut(hr, 0, H), 7: lambda: ht, 8: lambda: cut(hl, 0, H),
            }[m]()

        return src, dst

    def amp_refs(_):
        return (lambda m: amp9.at[4]), (lambda m: amp9.at[8 - m])

    def part_refs(it):
        return (lambda m: part.at[it, m]), (lambda m: got.at[it, 8 - m])

    def grad_refs(it):
        return (lambda m: grad_t.at[it]), (lambda m: grad9.at[it, 8 - m])

    nslot = ITERS * 2 * PAIRS
    zt = jnp.zeros((HALO + DMAX, 16, LANES), BF16)
    zh = jnp.zeros((3, rows + 2 * HALO, LANES), BF16)

    def clear(slot, _):
        halo_t[slot] = zt
        halo_b[slot] = zt
        halo_l[slot] = zh
        halo_r[slot] = zh
        return 0

    lax.fori_loop(0, nslot, clear, 0)
    z9 = jnp.zeros((9, 16, LANES), F32)
    amp9[...] = z9
    for it in range(ITERS):
        got[it] = z9
        grad9[it] = z9

    barrier = pltpu.get_barrier_semaphore()

    def greet(r, c):
        pl.semaphore_signal(barrier, inc=1, device_id=(r, c), device_id_type=MESH)

    for k in range(1, ncol):
        greet(my_r, lax.rem(my_c + k, ncol))
    for k in range(1, nrow):
        greet(lax.rem(my_r + k, nrow), my_c)
    greeted = (ncol - 1) + (nrow - 1)
    for m in (0, 2, 6, 8):
        there = exists(m)
        greeted = greeted + jnp.where(there, 1, 0)

        @pl.when(there)
        def _():
            greet(*ident(m))

    spread_ch = (
        lax.broadcasted_iota(jnp.int32, (16, LANES), 1) % 16 == lax.broadcasted_iota(jnp.int32, (16, LANES), 0)
    ).astype(F32).astype(BF16)
    wt_s[...] = jnp.dot(wt_ref[...], spread_ch, preferred_element_type=F32).reshape(2, LAYERS, 9, 16, LANES)
    pos = lax.broadcasted_iota(jnp.int32, (LANES, 16 * LANES), 0)
    col = lax.broadcasted_iota(jnp.int32, (LANES, 16 * LANES), 1)
    ee_s[...] = (pos == (col // LANES) * 8 + (col % LANES) // 16).astype(F32).astype(BF16)
    for t in range(9):
        b = blk_ref[8 - t]
        bh, bl = split2(b)
        bh, bl = bh.astype(F32), bl.astype(F32)
        bfw[t] = jnp.concatenate([bh, bh, bl], axis=0).astype(BF16)
        bbk[t] = jnp.concatenate([bh, bl, bh], axis=1).astype(BF16)

    amp9[4] = design_ref[...] * active_ref[...]
    new_ref[...] = design_ref[...]
    pl.semaphore_wait(barrier, greeted)
    amp_phase = ITERS * PER_ITER
    start(amp_phase, *amp_refs(0))

    lane = lax.broadcasted_iota(jnp.int32, (24, 16, LANES), 2) // 16
    jpos = lax.broadcasted_iota(jnp.int32, (24, 16, LANES), 0) - 8 - lane
    for l in range(LAYERS):
        d = dil_ref[l]
        masks = [jpos == rx * d for rx in (-1, 0, 1)]
        for f in range(2):
            for ry in range(3):
                acc = jnp.zeros((24, 16, LANES), F32)
                for rx in range(3):
                    acc = jnp.where(masks[rx], wt_s[f, l, 3 * ry + rx][None], acc)
                banded = acc.astype(BF16).reshape(384, LANES)
                wbig[f, l, 384 * ry : 384 * ry + 384] = banded
                wside[f, l, 0, 128 * ry : 128 * ry + 128] = banded[0:128]
                wside[f, l, 1, 128 * ry : 128 * ry + 128] = banded[256:384]
    ones_block = (
        lax.broadcasted_iota(jnp.int32, (LANES, LANES), 0) // 16
        == lax.broadcasted_iota(jnp.int32, (LANES, LANES), 1) // 16
    ).astype(F32).astype(BF16)

    lw = lanes_ref[0:1, :]
    lb = lanes_ref[1:2, :]
    ro = lanes_ref[2:3, :]

    def shifted(value, left=None, right=None):
        c0, c1 = value[:, 0:8], value[:, 8:16]
        bs = lax.broadcasted_iota(jnp.int32, c0.shape, 1)
        l0 = jnp.where(bs == 0, 0.0 if left is None else left[:, None, :], pltpu.roll(c1, 1, 1))
        r1 = jnp.where(bs == 7, 0.0 if right is None else right[:, None, :], pltpu.roll(c0, 7, 1))
        return (
            jnp.concatenate([l0, c0], axis=1).astype(BF16),
            value.astype(BF16),
            jnp.concatenate([c1, r1], axis=1).astype(BF16),
        )

    def put(ref, at, pieces):
        for n, piece in enumerate(pieces):
            ref[at : at + piece.shape[0], :, 128 * n : 128 * n + 128] = piece

    def conv_rows(ref, f, l, at, count):
        d = dil_ref[l]
        lhs = jnp.concatenate(
            [ref[pl.ds(at + (ry - 1) * d, count)].reshape(16 * count, 384) for ry in range(3)], axis=1
        )
        out = jnp.dot(lhs, wbig[f, l], preferred_element_type=F32)
        return out.reshape(count, 16, LANES)

    def f32(value):
        return value.astype(F32)

    tall = rows + 2 * DMAX

    def wide_conv(slot, phase, f, l, v3, extra=None):
        H, D, R = HALO, DMAX, rows
        refs = state_refs(slot, extra is not None)
        cf_s[H : H + R] = v3
        edge_t[slot, 0:H] = v3[0:H].astype(BF16)
        edge_b[slot, 0:H] = v3[R - H : R].astype(BF16)
        for n, (gl, gr) in enumerate(((0, 15), (8, 7))):
            edge_l[slot, n] = cf_s[H : H + R, gl, :].astype(BF16)
            edge_r[slot, n] = cf_s[H : H + R, gr, :].astype(BF16)
        if extra is not None:
            adj_s[...] = extra
            edge_t[slot, H : H + D] = extra[0:D].astype(BF16)
            edge_b[slot, H : H + D] = extra[R - D : R].astype(BF16)
            edge_l[slot, 2] = adj_s[:, 0, :].astype(BF16)
            edge_r[slot, 2] = adj_s[:, 15, :].astype(BF16)
        start(phase, *refs)
        put(xo, H, shifted(v3))
        mid = conv_rows(xo, f, l, H + D, R - 2 * D)
        arrive(phase, *refs)
        above, below = f32(halo_t[slot, 0:H]), f32(halo_b[slot, 0:H])
        cf_s[0:H] = above
        cf_s[H + R : 2 * H + R] = below
        put(xo, 0, shifted(above))
        put(xo, H + R, shifted(below))
        top = conv_rows(xo, f, l, H - D, 2 * D)
        bot = conv_rows(xo, f, l, H + R - D, 2 * D)
        side_s[0] = f32(halo_l[slot, 1])
        side_s[1] = f32(halo_l[slot, 0])
        side_s[2] = cf_s[:, 0, :]
        side_s[3] = cf_s[:, 15, :]
        side_s[4] = f32(halo_r[slot, 0])
        side_s[5] = f32(halo_r[slot, 1])
        d = dil_ref[l]
        near = ([], [])
        left, right = [], []
        for ry in range(3):
            six = [side_s[n, pl.ds(H - D + (ry - 1) * d, tall), :] for n in range(6)]
            for n in range(2):
                near[n].append(six[3 * n + 1])
            left += six[0:3]
            right += six[3:6]
        lhs = jnp.concatenate(
            [jnp.concatenate(left, axis=1), jnp.concatenate(right, axis=1)], axis=0
        ).astype(BF16)
        outer = jnp.dot(lhs, wbig[f, l], preferred_element_type=F32)
        inner = [
            jnp.dot(
                jnp.concatenate(near[n], axis=1).astype(BF16), wside[f, l, n], preferred_element_type=F32
            )
            for n in range(2)
        ]
        bs = lax.broadcasted_iota(jnp.int32, (tall, 8, LANES), 1)
        add0 = jnp.where(bs == 0, inner[0][:, None, :], 0.0)
        add1 = jnp.where(bs == 7, inner[1][:, None, :], 0.0)
        out = jnp.concatenate([top, mid, bot], axis=0) + jnp.concatenate([add0, add1], axis=1)
        return out, outer[0:tall], outer[tall : 2 * tall]

    inside = [jnp.where(exists(m), 1.0, 0.0).astype(F32) for m in (1, 7, 3, 5)]

    def clip_map(value):
        D, R = DMAX, rows
        return jnp.concatenate(
            [value[0:D] * inside[0], value[D : D + R], value[D + R : 2 * D + R] * inside[1]], axis=0
        )

    def near_conv(f, l, c3, left, right):
        put(xn, 0, shifted(clip_map(c3), clip_map(left) * inside[2], clip_map(right) * inside[3]))
        return conv_rows(xn, f, l, DMAX, rows)

    def sigmoid(v):
        return 0.5 + 0.5 * jnp.tanh(0.5 * v)

    def silu_and_slope(v):
        s = sigmoid(v)
        return v * s, s * (1.0 + v * (1.0 - s))

    def render(amp, dest):
        high, low = split2(amp.reshape(144, LANES))
        high, low = high.astype(F32), low.astype(F32)
        packed = (high + pltpu.roll(low, 16, 1) + pltpu.roll(high, 32, 1)).astype(BF16)
        picked = jnp.dot(sel_ref[...], packed, preferred_element_type=F32).astype(BF16)
        height = None
        for t in range(9):
            term = jnp.dot(picked[16 * t : 16 * t + 16, 0:48], bfw[t], preferred_element_type=F32)
            height = term if height is None else height + term
        two = jnp.concatenate([height[:, 0:128], height[:, 128:256]], axis=0)
        high, low = split2(two)
        spread = jnp.dot(high, ee_s[...], preferred_element_type=F32)
        spread = spread + jnp.dot(low, ee_s[...], preferred_element_type=F32)
        for s in range(2):
            for k in range(16):
                q = 16 * s + k
                y, xh = q // 2, q % 2
                for a in range(rows // 16):
                    dest[16 * a + y, 8 * xh : 8 * xh + 8, :] = spread[
                        16 * s + 8 * a : 16 * s + 8 * a + 8, 128 * k : 128 * k + 128
                    ]

    arrive(amp_phase, *amp_refs(0))
    render(amp9[...], h_s)
    sent(amp_phase, *amp_refs(0))

    def step(it, _):
        base = it * PER_ITER
        slot0 = it * 2 * PAIRS
        D, R = DMAX, rows
        state = f32((lw * h_s[...] + lb + f32(film_ref[...])).astype(BF16))
        for n in range(PAIRS):
            la, lb_ = 2 * n, 2 * n + 1
            bias = lanes_ref[4 + la : 5 + la, :]
            outs = wide_conv(slot0 + n, base + n, 0, la, state)
            olds = (cf_s[D : D + tall], side_s[1, D : D + tall], side_s[4, D : D + tall])
            news = []
            for k in range(3):
                pre = outs[k] + bias
                gain, steep = silu_and_slope(pre)
                if k == 0:
                    steep_c[n] = steep
                else:
                    steep_w[n, k - 1] = steep
                news.append(f32((olds[k] + gain).astype(BF16)))
            pre = near_conv(0, lb_, *news) + lanes_ref[4 + lb_ : 5 + lb_, :]
            gain, steep = silu_and_slope(pre)
            steep_o[n] = steep
            state = f32((news[0][D : D + R] + gain).astype(BF16))
        pressure = None
        for piece in split2((ro * state).reshape(nx, LANES)):
            term = jnp.dot(piece, ones_block, preferred_element_type=F32)
            pressure = term if pressure is None else pressure + term
        misfit = pressure - target_ref[...].reshape(nx, LANES)
        miss = jnp.sum(misfit * misfit, keepdims=True) * (0.5 / 16)
        adjoint = (ro * (misfit * (1.0 / 256.0))).reshape(rows, 16, LANES)

        def slope_of(grad, steep):
            return f32((grad * steep).astype(BF16))

        for n in range(PAIRS):
            pair = PAIRS - 1 - n
            slot = slot0 + PAIRS + n
            slope = slope_of(adjoint, steep_o[pair])
            outs = wide_conv(slot, base + PAIRS + n, 1, 2 * pair + 1, slope, adjoint)
            grown = jnp.concatenate(
                [f32(halo_t[slot, HALO : HALO + D]), adjoint, f32(halo_b[slot, HALO : HALO + D])], axis=0
            )
            adjs = (
                grown + outs[0],
                f32(halo_l[slot, 2])[D : D + tall] + outs[1],
                f32(halo_r[slot, 2])[D : D + tall] + outs[2],
            )
            pres = (steep_c[pair], steep_w[pair, 0], steep_w[pair, 1])
            slopes = [slope_of(x, v) for x, v in zip(adjs, pres)]
            adjoint = adjs[0][D : D + R] + near_conv(1, 2 * pair, *slopes)
        adj_s[...] = lw * adjoint
        strips = []
        for s in range(2):
            tiles = []
            for k in range(16):
                q = 16 * s + k
                y, xh = q // 2, q % 2
                tiles.append(
                    jnp.concatenate(
                        [adj_s[16 * a + y, 8 * xh : 8 * xh + 8, :] for a in range(rows // 16)], axis=0
                    )
                )
            strips.append(jnp.concatenate(tiles, axis=1))
        both = jnp.concatenate(strips, axis=0)
        folded = None
        for piece in split2(both):
            term = lax.dot_general(piece, ee_s[...], (((1,), (1,)), ((), ())), preferred_element_type=F32)
            folded = term if folded is None else folded + term
        hg = jnp.concatenate([folded[0:16], folded[16:32]], axis=1)
        high, low = split2(hg)
        wide = jnp.concatenate([high, high, low], axis=1)
        q_s[...] = jnp.zeros((144, LANES), F32)
        for t in range(9):
            q_s[16 * t : 16 * t + 16, 0:16] = lax.dot_general(
                wide, bbk[t], (((1,), (1,)), ((), ())), preferred_element_type=F32
            )
        mine = None
        for piece in split2(q_s[...]):
            term = jnp.dot(selt_ref[...], piece, preferred_element_type=F32)
            mine = term if mine is None else mine + term
        mine = mine.reshape(9, 16, LANES)
        part[it] = mine
        p_phase = base + 2 * PAIRS
        start(p_phase, *part_refs(it))
        got[it, 4] = mine[4]
        arrive(p_phase, *part_refs(it))
        gradient = jnp.sum(got[it], axis=0) * active_ref[...]
        squares = jnp.sum(gradient * gradient, keepdims=True)
        sub = lax.broadcasted_iota(jnp.int32, (8, LANES), 0)
        tile = jnp.where(sub == 0, squares, miss)
        ar1_src[it] = tile
        g_phase = p_phase + 1

        def ring(n, src, dst, dev):
            return pltpu.make_async_remote_copy(
                src_ref=src.at[it], dst_ref=dst,
                send_sem=ar_send.at[it, n], recv_sem=ar_recv.at[it, n],
                device_id=dev, device_id_type=MESH,
            )

        for k in range(1, ncol):
            ring(0, ar1_src, ar1.at[it, my_c], (my_r, lax.rem(my_c + k, ncol))).start()
        ar1[it, my_c] = tile
        more = it < ITERS - 1

        @pl.when(more)
        def _():
            grad_t[it] = gradient
            start(g_phase, *grad_refs(it))
            grad9[it, 4] = gradient

        many = ar1.at[it, pl.ds(0, ncol - 1)]
        pltpu.make_async_copy(many, many, ar_recv.at[it, 0]).wait()
        tile2 = jnp.sum(ar1[it], axis=0)
        ar2_src[it] = tile2
        for k in range(1, nrow):
            ring(1, ar2_src, ar2.at[it, my_r], (lax.rem(my_r + k, nrow), my_c)).start()
        ar2[it, my_r] = tile2

        @pl.when(more)
        def _():
            arrive(g_phase, *grad_refs(it))
            render(grad9[it], hd_s)

        many = ar2.at[it, pl.ds(0, nrow - 1)]
        pltpu.make_async_copy(many, many, ar_recv.at[it, 1]).wait()
        total = jnp.sum(ar2[it], axis=0)
        scale = step_rate / jnp.sqrt(total[0:1] * (1.0 / total_entries) + norm_eps)
        obj_ref[it] = jnp.sum(total[1:2, 0:1]) * (1.0 / total_cells)
        new_ref[...] = new_ref[...] - gradient * scale

        @pl.when(more)
        def _():
            h_s[...] = h_s[...] - hd_s[...] * scale[None]

        return 0

    lax.fori_loop(0, ITERS, step, 0)

    def drain(it, _):
        base = it * PER_ITER
        for n in range(2 * PAIRS):
            sent(base + n, *state_refs(it * 2 * PAIRS + n, n >= PAIRS))
        sent(base + 2 * PAIRS, *part_refs(it))

        @pl.when(it < ITERS - 1)
        def _():
            sent(base + 2 * PAIRS + 1, *grad_refs(it))

        many = ar1.at[it, pl.ds(0, ncol - 1)]
        pltpu.make_async_copy(many, many, ar_send.at[it, 0]).wait()
        many = ar2.at[it, pl.ds(0, nrow - 1)]
        pltpu.make_async_copy(many, many, ar_send.at[it, 1]).wait()
        return 0

    lax.fori_loop(0, ITERS, drain, 0)


def select_matrix(dr_count, dc_count):
    sel = np.zeros((9, dr_count, dc_count, 9, dr_count, dc_count), np.float32)
    for t, (ry, rx) in enumerate(tap_list()):
        for a in range(dr_count):
            for b in range(dc_count):
                ta, tb = a + ry, b + rx
                nr, nc = ta // dr_count, tb // dc_count
                sel[t, a, b, 3 * (nr + 1) + nc + 1, ta - nr * dr_count, tb - nc * dc_count] = 1
    size = 9 * dr_count * dc_count
    return sel.reshape(size, size)


def basis_blocks(stamp_basis):
    nparams, side = stamp_basis.shape[0], stamp_basis.shape[1] // 2
    half = side // 2
    padded = jnp.pad(stamp_basis, ((0, 16 - nparams), (half, half), (half, half)))
    windows = padded.reshape(16, 3, side, 3, side).transpose(1, 3, 0, 2, 4)
    return windows.reshape(9, 16, side * side)


def on_device(
    design, active, stamp_basis, film_field, lift_weight, lift_bias, conv_weight, conv_bias, readout, target, dilation
):
    channels, rows, cols = film_field.shape
    nparams, drows, dcols = design.shape
    nrow = lax.axis_size("rows")
    ncol = lax.axis_size("cols")
    ndev = nrow * ncol
    total_cells = rows * cols * ndev
    total_entries = nparams * drows * dcols * ndev

    def by_dimple(v):
        v = v.reshape(nparams, drows * dcols).T
        return jnp.pad(v, ((0, 0), (0, LANES - nparams)))

    design_t = by_dimple(design)
    active_t = jnp.broadcast_to(active.astype(F32).reshape(drows * dcols, 1), (drows * dcols, LANES))
    film = film_field.reshape(channels, rows, dcols, 2, 8).transpose(1, 3, 2, 4, 0).reshape(rows, 16, LANES)
    targ = target.reshape(rows, dcols, 2, 8).transpose(0, 2, 1, 3).reshape(rows, 16, 8, 1)
    targ = jnp.broadcast_to(targ, (rows, 16, 8, 16)).reshape(rows, 16, LANES)
    lanes = jnp.concatenate(
        [jnp.tile(jnp.stack([lift_weight, lift_bias, readout, readout]), (1, 8)), jnp.tile(conv_bias, (1, 8))]
    )
    wt = jnp.stack([jnp.swapaxes(conv_weight, 2, 3), conv_weight[:, ::-1]])
    wt = wt.reshape(2 * LAYERS * 9 * channels, channels)
    blocks = basis_blocks(stamp_basis)
    sel = select_matrix(drows, dcols).astype(BF16)

    nslot = ITERS * 2 * PAIRS
    phases = ITERS * PER_ITER + 1
    tall = rows + 2 * DMAX
    vmem = pl.BlockSpec(memory_space=pltpu.VMEM)
    new, obj = pl.pallas_call(
        functools.partial(kernel, (nrow, ncol, rows, total_cells, total_entries)),
        out_shape=(
            jax.ShapeDtypeStruct((16, LANES), F32),
            jax.ShapeDtypeStruct((ITERS,), F32),
        ),
        in_specs=[pl.BlockSpec(memory_space=pltpu.SMEM)] + [vmem] * 9,
        out_specs=(vmem, pl.BlockSpec(memory_space=pltpu.SMEM)),
        scratch_shapes=[
            pltpu.VMEM((nslot, HALO + DMAX, 16, LANES), BF16),
            pltpu.VMEM((nslot, HALO + DMAX, 16, LANES), BF16),
            pltpu.VMEM((nslot, HALO + DMAX, 16, LANES), BF16),
            pltpu.VMEM((nslot, HALO + DMAX, 16, LANES), BF16),
            pltpu.VMEM((nslot, 3, rows, LANES), BF16),
            pltpu.VMEM((nslot, 3, rows, LANES), BF16),
            pltpu.VMEM((nslot, 3, rows + 2 * HALO, LANES), BF16),
            pltpu.VMEM((nslot, 3, rows + 2 * HALO, LANES), BF16),
            pltpu.VMEM((rows + 2 * HALO, 16, LANES), F32),
            pltpu.VMEM((6, rows + 2 * HALO, LANES), F32),
            pltpu.VMEM((rows + 2 * HALO, 16, 384), BF16),
            pltpu.VMEM((tall, 16, 384), BF16),
            pltpu.VMEM((2, LAYERS, 3 * 384, LANES), BF16),
            pltpu.VMEM((2, LAYERS, 2, 384, LANES), BF16),
            pltpu.VMEM((2, LAYERS, 9, 16, LANES), F32),
            pltpu.VMEM((PAIRS, rows, 16, LANES), F32),
            pltpu.VMEM((PAIRS, tall, 16, LANES), F32),
            pltpu.VMEM((PAIRS, 2, tall, LANES), F32),
            pltpu.VMEM((rows, 16, LANES), F32),
            pltpu.VMEM((LANES, 16 * LANES), BF16),
            pltpu.VMEM((9, 48, 256), BF16),
            pltpu.VMEM((9, 16, 768), BF16),
            pltpu.VMEM((rows, 16, LANES), F32),
            pltpu.VMEM((rows, 16, LANES), F32),
            pltpu.VMEM((9, 16, LANES), F32),
            pltpu.VMEM((ITERS, 9, 16, LANES), F32),
            pltpu.VMEM((ITERS, 9, 16, LANES), F32),
            pltpu.VMEM((ITERS, 9, 16, LANES), F32),
            pltpu.VMEM((144, LANES), F32),
            pltpu.VMEM((ITERS, 16, LANES), F32),
            pltpu.VMEM((ITERS, ncol, 8, LANES), F32),
            pltpu.VMEM((ITERS, 8, LANES), F32),
            pltpu.VMEM((ITERS, nrow, 8, LANES), F32),
            pltpu.VMEM((ITERS, 8, LANES), F32),
            pltpu.SemaphoreType.DMA((phases, 9)),
            pltpu.SemaphoreType.DMA((phases, 9)),
            pltpu.SemaphoreType.DMA((ITERS, 2)),
            pltpu.SemaphoreType.DMA((ITERS, 2)),
        ],
        compiler_params=pltpu.CompilerParams(
            collective_id=0, has_side_effects=True, vmem_limit_bytes=40 * 1024 * 1024
        ),
    )(dilation, design_t, active_t, film, targ, lanes, wt, blocks, sel, sel.T)
    new_design = new[:, :nparams].T.reshape(nparams, drows, dcols)
    return new_design, obj


def solution(mesh):
    placed = (
        P(None, "rows", "cols"),
        P("rows", "cols"),
        P(),
        P(None, "rows", "cols"),
        P(),
        P(),
        P(),
        P(),
        P(),
        P("rows", "cols"),
        P(),
    )
    return jax.shard_map(
        on_device,
        mesh=mesh,
        in_specs=placed,
        out_specs=(P(None, "rows", "cols"), P()),
        check_vma=False,
    )
```
